32 devices in a mesh: section: 2 (over x), win: 4 (over y, core), dp: 4 (over z).
Axes of the slice: x: 2, y: 2, z: 4, core: 2. Of those that a mesh axis runs over, the one named last changes fastest.
Arguments:
- tokens: bfloat16 [2, 4, 4, 64, 1536], P(None, 'win', 'dp'), may hold values from -6 to 6
- regions: int32 [2, 4, 256], P('section', 'win'), may hold values from 0 to 3
- norm_gain: float32 [2, 1536], P('section'), may hold values from 0.1 to 1.9
- qkv_weight: bfloat16 [2, 1536, 3, 1024], P('section', None, None, 'dp'), as said below
- out_weight: bfloat16 [2, 1024, 1536], P('section', 'dp'), may hold values from -2 to 2
- final_gain: float32 [1536], replicated, may hold values from 0.1 to 1.9
- dec_weight: bfloat16 [1536, 1104], P(None, 'section'), may hold values from -0.15625 to 0.15625
Outputs:
- decoded: bfloat16 [2, 4, 4, 64, 1104], P(None, 'win', 'dp', None, 'section')
The draws below stay inside these ranges and needn't reach their ends.
Inputs may be any that keep to these rules, and one draw needn't show every extreme that they name: `qkv_weight`: entries lie below 80 / sqrt(1536) in magnitude.
All inputs are finite; a program needn't handle non-finite values.
Results may differ from the reference program's by a relative error of at most 0.03.
Values may be sent and summed in bfloat16 or wider, within the bound.
A program may use at most 64 MiB of HBM per device.

```python
import math
import jax
import jax.numpy as jnp
import numpy as np
from jax import lax

D = 1536
HEADS = 16
HEAD_DIM = 64
DEC = 1104
QUAD = 64
MICRO = 2
LAYERS = 2
WINDOWS = 4


def draw_qkv_weight(key, part):
    parts_keys = jax.random.split(key, 1)
    shape = (LAYERS, D, 3, HEADS, HEAD_DIM)
    full = jax.random.truncated_normal(parts_keys[0], -4.0, 4.0, shape, jnp.float32) / math.sqrt(D)
    return full.reshape(LAYERS, D, 3, HEADS * HEAD_DIM).astype(jnp.bfloat16)


def set_ends(entries, rng, smallest, high):
    longest = entries.shape.index(max(entries.shape))
    spots = []
    for shift in (0, 1):
        where = [jax.random.randint(jax.random.fold_in(rng, axis), (), 0, length) for axis, length in enumerate(entries.shape)]
        where[longest] = (where[longest] + shift) % entries.shape[longest]
        spots.append(tuple(where))
    return entries.at[spots[0]].set(smallest).at[spots[1]].set(high)


def steps_of(key, dims, shards, smallest, high):
    def one(axis_at, blocks):
        steps = jax.random.uniform(jax.random.fold_in(jax.random.fold_in(key, 6), axis_at), (blocks,), jnp.float32, smallest / len(shards), high / len(shards))
        return jnp.repeat(jnp.exp(steps), dims[axis_at] // blocks).reshape((-1,) + (1,) * (len(dims) - axis_at - 1))

    gain = one(*shards[0])
    for cut in shards[1:]:
        gain = gain * one(*cut)
    return gain


def rank_bounds(count, skew):
    weights = [(1 << 20) // math.isqrt(grade ** skew) + 1 for grade in range(1, count + 1)]
    width = 1 + sum(weights) // (1 << 30)
    return np.cumsum(np.array([max(1, weight // width) for weight in weights]))


def skewed_ids(key, shape, amount, slope):
    listing = rank_bounds(amount, slope)
    pick = jax.random.randint(jax.random.fold_in(key, 1), shape, 0, int(listing[amount - 1]))
    grade = jnp.searchsorted(jnp.asarray(listing, jnp.int32), pick, side="right")
    return jax.random.permutation(jax.random.fold_in(key, 2), amount)[grade].astype(jnp.int32)


def normal_values(stream_key, shape, width, reach, shards=(), kind=jnp.bfloat16):
    values = jax.random.normal(stream_key, shape, jnp.float32) * width
    if len(shards) > 0:
        values = steps_of(stream_key, shape, shards, -0.22, 0.18) * values
    return jnp.clip(values, min=-reach, max=reach).astype(kind)


def setup_inputs(seed: int = 0) -> dict:
    streams_of = jax.random.split(jax.random.key(seed), 8)
    return {
        "tokens": normal_values(streams_of[0], (MICRO, WINDOWS, 4, QUAD, D), 1.0, 6.0, ((1, 4), (2, 4))),
        "regions": set_ends(skewed_ids(streams_of[1], (LAYERS, WINDOWS, 4 * QUAD), 4, 2), jax.random.fold_in(streams_of[1], 3), 0, 3).astype(jnp.int32),
        "norm_gain": jnp.clip(1.0 + 0.18 * jax.random.normal(streams_of[2], (LAYERS, D), jnp.float32), 0.1, 1.9),
        "qkv_weight": draw_qkv_weight(jax.random.fold_in(streams_of[7], 71), 0),
        "out_weight": normal_values(streams_of[4], (LAYERS, HEADS * HEAD_DIM, D), 0.15, 2.0, ((0, 2), (1, 4))),
        "final_gain": jnp.clip(1.0 + 0.18 * jax.random.normal(streams_of[5], (D,), jnp.float32), 0.1, 1.9),
        "dec_weight": normal_values(streams_of[6], (D, DEC), D ** -0.5, 0.15625, ((1, 2),)),
    }


def normalize(hidden, scales):
    values = hidden.astype(jnp.float32)
    center = values - lax.optimization_barrier(jnp.mean(values, axis=-1, keepdims=True))
    spread = lax.optimization_barrier(jnp.mean(center * center, axis=-1, keepdims=True))
    return (center * lax.rsqrt(spread + 1e-05) * scales).astype(jnp.bfloat16)

def rounded(values):
    return lax.optimization_barrier(values.astype(jnp.bfloat16)).astype(jnp.float32)

def attend(projected, labels):
    row_count = projected.shape[0]
    queries = projected[:, 0].reshape(row_count, HEADS, HEAD_DIM).astype(jnp.float32)
    keys_all = projected[:, 1].reshape(row_count, HEADS, HEAD_DIM).astype(jnp.float32)
    values_all = projected[:, 2].reshape(row_count, HEADS, HEAD_DIM).astype(jnp.float32)
    scores = jnp.einsum('qhe,khe->hqk', queries, keys_all) / jnp.sqrt(jnp.float32(HEAD_DIM))
    allowed = labels[:, None] == labels[None, :]
    scores = jnp.where(allowed[None], scores, -jnp.inf)
    largest = lax.optimization_barrier(jnp.max(scores, axis=-1, keepdims=True))
    weights = jnp.exp(scores - largest)
    shares = (weights / lax.optimization_barrier(jnp.sum(weights, axis=-1, keepdims=True))).astype(jnp.bfloat16)
    blended = jnp.einsum('hqk,khe->qhe', shares.astype(jnp.float32), values_all)
    return blended.astype(jnp.bfloat16).reshape(row_count, HEADS * HEAD_DIM)

def reference(tokens, regions, norm_gain, qkv_weight, out_weight, final_gain, dec_weight):
    windows = tokens.shape[1]
    block = HEADS * HEAD_DIM // 4
    half = QUAD // 2

    def layer(hidden, labels_all, scales, projection, out_matrix):
        normed = normalize(hidden, scales).reshape(windows, 4 * QUAD, D)
        projected = jnp.einsum('wtd,dcf->wtcf', normed.astype(jnp.float32), projection.astype(jnp.float32)).astype(jnp.bfloat16)

        def one_window(items):
            window_proj, labels = items
            blended = attend(window_proj, labels)
            total = jnp.zeros((4 * QUAD, D), jnp.float32)
            for source in range(4):
                total = total + rounded(jnp.dot(blended[:, source * block:(source + 1) * block], out_matrix[source * block:(source + 1) * block], preferred_element_type=jnp.float32))
            return total
        update = lax.map(one_window, (projected, labels_all))
        return (hidden.astype(jnp.float32) + update.reshape(windows, 4, QUAD, D)).astype(jnp.bfloat16)
    outputs = []
    for micro_index in range(MICRO):
        hidden = tokens[micro_index]
        for layer_index in range(LAYERS):
            hidden = layer(hidden, regions[layer_index], norm_gain[layer_index], qkv_weight[layer_index], out_weight[layer_index])
            hidden = jnp.concatenate([hidden[:, :, half:], jnp.roll(hidden[:, :, :half], -1, axis=0)], axis=2)
        final = normalize(hidden, final_gain)
        result = jnp.dot(final.reshape(-1, D), dec_weight, preferred_element_type=jnp.float32)
        outputs.append(result.astype(jnp.bfloat16).reshape(windows, 4, QUAD, DEC))
    return jnp.stack(outputs)
```

```python
import functools
import math

import jax
import jax.numpy as jnp
from jax import lax
from jax.experimental import pallas as pl
from jax.experimental.pallas import tpu as pltpu
from jax.sharding import PartitionSpec as P

HEAD_DIM = 64
MESH = pl.DeviceIdType.MESH
EXCLUDED = -1e30


def normalize(hidden, scales):
    values = hidden.astype(jnp.float32)
    center = values - jnp.mean(values, axis=-1, keepdims=True)
    spread = jnp.mean(center * center, axis=-1, keepdims=True)
    return (center * lax.rsqrt(spread + 1e-05) * scales).astype(jnp.bfloat16)


def kernel(
    sections, windows, bands,
    tokens, labels, gain, wqkv_hbm, wout_hbm, final_gain, wdec_hbm,
    decoded,
    full, relay, normed, projected, wqkv, wout, wdec, bias, bstage, blend, hstage, fstage, final,
    ag_send, ag_recv, a2a_send, a2a_recv, hid_send, hid_recv, fin_send, fin_recv,
    rel_send, rel_recv, fwd_send, wz_send, wz_recv, wy_send, wy_recv, wc_send, wc_recv, load_sem,
):
    micros, quad, width = tokens.shape
    half = quad // 2
    last = sections - 1
    s = lax.axis_index("section")
    w = lax.axis_index("win")
    b = lax.axis_index("dp")
    before = lax.rem(w + windows - 1, windows)
    after = lax.rem(w + 1, windows)
    core_peer = w + 1 - 2 * lax.rem(w, 2)
    chip_peer = w + 2 - 4 * lax.rem(w // 2, 2)
    quarter = lax.rem(w, 4)
    group_rows = wout_hbm.shape[0]
    piece = group_rows // 4

    def band(k):
        return lax.rem(b + k, bands)

    def send(src, dst, send_sem, recv_sem, device):
        return pltpu.make_async_remote_copy(
            src_ref=src, dst_ref=dst, send_sem=send_sem, recv_sem=recv_sem,
            device_id=device, device_id_type=MESH,
        )

    def ag_copy(m, k):
        return send(full.at[m, b], full.at[m, b], ag_send.at[m, k - 1],
                    ag_recv.at[m, bands - k - 1], (s, w, band(k)))

    def ag_arrival(m, k):
        slot = full.at[m, band(k)]
        return send(slot, slot, ag_send.at[m, k - 1], ag_recv.at[m, k - 1], (s, w, band(k)))

    def relay_copy(k):
        return send(relay.at[b], relay.at[b], rel_send.at[k - 1],
                    rel_recv.at[bands - k - 1], (s, w, band(k)))

    def relay_arrival(k):
        slot = relay.at[band(k)]
        return send(slot, slot, rel_send.at[k - 1], rel_recv.at[k - 1], (s, w, band(k)))

    def forward_copy(k):
        return send(relay.at[band(k)], full.at[1, band(k)], fwd_send.at[k - 1],
                    ag_recv.at[1, k - 1], (0, w, b))

    def a2a_copy(m, k):
        return send(bstage.at[m, band(k)], blend.at[m, b], a2a_send.at[m, k - 1],
                    a2a_recv.at[m, bands - k - 1], (s, w, band(k)))

    def a2a_arrival(m, k):
        slot = blend.at[m, band(k)]
        return send(slot, slot, a2a_send.at[m, k - 1], a2a_recv.at[m, k - 1], (s, w, band(k)))

    def wz_copy(k):
        rows = pl.ds(pl.multiple_of(quarter * piece, piece), piece)
        return send(wout_hbm.at[rows], wout.at[b, rows], wz_send.at[k - 1],
                    wz_recv.at[bands - k - 1], (s, w, band(k)))

    def w_piece(k, owner):
        return wout.at[band(k), pl.ds(pl.multiple_of(lax.rem(owner, 4) * piece, piece), piece)]

    def wz_arrival(k):
        slot = w_piece(k, w)
        return send(slot, slot, wz_send.at[k - 1], wz_recv.at[k - 1], (s, w, band(k)))

    def wy_copy(k):
        slot = w_piece(k, w)
        return send(slot, slot, wy_send.at[k - 1], wy_recv.at[k - 1], (s, chip_peer, b))

    def wy_arrival(k):
        slot = w_piece(k, chip_peer)
        return send(slot, slot, wy_send.at[k - 1], wy_recv.at[k - 1], (s, chip_peer, b))

    def wc_copy(k, far):
        slot = w_piece(k, chip_peer if far else w)
        index = 3 * far + k - 1
        return send(slot, slot, wc_send.at[index], wc_recv.at[index], (s, core_peer, b))

    def wc_arrival(k, far):
        other = core_peer + 2 - 4 * lax.rem(core_peer // 2, 2)
        slot = w_piece(k, other if far else core_peer)
        index = 3 * far + k - 1
        return send(slot, slot, wc_send.at[index], wc_recv.at[index], (s, core_peer, b))

    def hidden_copy(m, part):
        rows_from = pl.ds(half * (1 - part), half)
        rows_to = pl.ds(half * part, half)
        return send(hstage.at[m, rows_from], full.at[m, b, rows_to], hid_send.at[m, part],
                    hid_recv.at[m, part], (s + 1, before if part else w, b))

    def hidden_arrival(m, part):
        slot = full.at[m, b, pl.ds(half * part, half)]
        return send(slot, slot, hid_send.at[m, part], hid_recv.at[m, part], (s, after, b))

    def final_copy(m, to, part):
        rows_from = pl.ds(half * (1 - part), half)
        rows_to = pl.ds(half * part, half)
        return send(fstage.at[m, rows_from], final.at[m, rows_to], fin_send.at[m, to, part],
                    fin_recv.at[m, part], (to, before if part else w, b))

    def final_arrival(m, part):
        slot = final.at[m, pl.ds(half * part, half)]
        return send(slot, slot, fin_send.at[m, 0, part], fin_recv.at[m, part], (s, after, b))

    others = range(1, bands)

    load_qkv = pltpu.make_async_copy(wqkv_hbm, wqkv, load_sem.at[0])
    load_out = pltpu.make_async_copy(wout_hbm, wout.at[b], load_sem.at[1])
    load_dec = pltpu.make_async_copy(wdec_hbm, wdec, load_sem.at[2])
    load_qkv.start()
    load_out.start()
    load_dec.start()

    barrier = pltpu.get_barrier_semaphore()
    partners = [(s, w, band(k)) for k in others]
    partners += [(s, core_peer, b), (s, chip_peer, b)]
    partners += [(lax.rem(s + k, sections), w, b) for k in range(1, sections)]
    for to in range(sections):
        partners += [(to, before, b), (to, after, b)]
    for device in partners:
        pl.semaphore_signal(barrier, inc=1, device_id=device, device_id_type=MESH)

    @pl.when(s == 0)
    def _():
        for m in range(micros):
            full[m, b] = tokens[m]

    @pl.when(s == 1)
    def _():
        relay[b] = tokens[1]

    pl.semaphore_wait(barrier, len(partners))

    def start_gather(m):
        @pl.when(s > 0)
        def _():
            for part in range(2):
                hidden_arrival(m, part).wait_recv()

        if m == 1:
            @pl.when(s > 0)
            def _():
                for k in others:
                    ag_copy(m, k).start()
        else:
            for k in others:
                ag_copy(m, k).start()

    def start_weights():
        for k in others:
            wz_copy(k).start()

    def weights_over_chips():
        for k in others:
            wz_arrival(k).wait_recv()
            wy_copy(k).start()
            wc_copy(k, 0).start()

    def weights_over_cores():
        for k in others:
            wy_arrival(k).wait_recv()
            wc_copy(k, 1).start()

    def weights_all():
        for k in others:
            wc_arrival(k, 0).wait_recv()
            wc_arrival(k, 1).wait_recv()

    def normalize_band(m, slot):
        rows = pl.ds(pl.multiple_of(slot * quad, quad), quad)
        normed[rows, :] = normalize(full[m, slot], gain[...])

    def project(m):
        normalize_band(m, b)
        for k in others:
            ag_arrival(m, k).wait_recv()
            normalize_band(m, band(k))
        if m == 0:
            load_qkv.wait()
        for c in range(3):
            projected[c] = jnp.dot(
                normed[...], wqkv[c], preferred_element_type=jnp.float32
            ).astype(jnp.bfloat16)

    def attend(m):
        inner = projected.shape[2]
        rows = projected.shape[1]
        lane = lax.broadcasted_iota(jnp.int32, (rows, 128), 1)
        for pair in range(inner // 128):
            columns = slice(128 * pair, 128 * pair + 128)
            queries = projected[0, :, columns]
            keys_all = projected[1, :, columns]
            values_all = projected[2, :, columns]
            results = []
            for side in range(128 // HEAD_DIM):
                mine = (lane // HEAD_DIM) == side
                query = jnp.where(mine, queries, jnp.zeros_like(queries))
                scores = lax.dot_general(
                    query, keys_all, (((1,), (1,)), ((), ())), preferred_element_type=jnp.float32
                ) * (1.0 / math.sqrt(HEAD_DIM)) + bias[...]
                largest = jnp.max(scores, axis=-1, keepdims=True)
                weights = jnp.exp(scores - largest)
                total = jnp.sum(weights, axis=-1, keepdims=True)
                product = jnp.dot(
                    weights.astype(jnp.bfloat16), values_all, preferred_element_type=jnp.float32
                )
                results.append(product / total)
            mixed = results[0]
            for side in range(1, 128 // HEAD_DIM):
                mixed = jnp.where((lane // HEAD_DIM) == side, results[side], mixed)
            mixed = mixed.astype(jnp.bfloat16)
            for place in range(bands):
                bstage[m, place, :, columns] = mixed[place * quad:(place + 1) * quad]
        for k in others:
            a2a_copy(m, k).start()
        blend[m, b] = bstage[m, b]

    def finish(m):
        for k in others:
            a2a_arrival(m, k).wait_recv()
        for start in range(0, width, 512):
            columns = slice(start, start + 512)
            total = full[m, b, :, columns].astype(jnp.float32)
            for group in range(bands):
                total += jnp.dot(
                    blend[m, group], wout[group, :, columns], preferred_element_type=jnp.float32
                )
            hstage[m, :, columns] = total.astype(jnp.bfloat16)

        @pl.when(s < last)
        def _():
            for part in range(2):
                hidden_copy(m, part).start()

        @pl.when(s == last)
        def _():
            fstage[m] = normalize(hstage[m], final_gain[...])
            for to in range(sections):
                final_copy(m, to, 1).start()
                if to != last:
                    final_copy(m, to, 0).start()
            final[m, :half] = fstage[m, half:]

    def decode(m):
        @pl.when(s < last)
        def _():
            final_arrival(m, 0).wait_recv()

        final_arrival(m, 1).wait_recv()
        decoded[m] = lax.dot_general(
            final[m], wdec[...], (((1,), (1,)), ((), ())), preferred_element_type=jnp.float32
        ).astype(jnp.bfloat16)

    @pl.when(s == 1)
    def _():
        for k in others:
            relay_copy(k).start()

    @pl.when(s > 0)
    def _():
        start_weights()

    row = labels[...].astype(jnp.float32)
    across = jnp.broadcast_to(row, bias.shape)
    bias[...] = jnp.where(across == across.T, 0.0, EXCLUDED)

    @pl.when(s == 1)
    def _():
        for k in others:
            relay_arrival(k).wait_recv()
            forward_copy(k).start()

    @pl.when(s > 0)
    def _():
        weights_over_chips()
        weights_over_cores()

    start_gather(0)

    @pl.when(s == 0)
    def _():
        start_weights()

    project(0)
    start_gather(1)

    @pl.when(s == 0)
    def _():
        weights_over_chips()

    attend(0)

    @pl.when(s == 0)
    def _():
        weights_over_cores()

    load_out.wait()
    weights_all()
    finish(0)
    project(1)
    attend(1)
    finish(1)
    load_dec.wait()
    decode(0)
    decode(1)

    for m in range(micros):
        for k in others:
            a2a_copy(m, k).wait_send()
            if m != 1:
                ag_copy(m, k).wait_send()
    for k in others:
        wz_copy(k).wait_send()
        wy_copy(k).wait_send()
        wc_copy(k, 0).wait_send()
        wc_copy(k, 1).wait_send()

    @pl.when(s > 0)
    def _():
        for k in others:
            ag_copy(1, k).wait_send()

    @pl.when(s == 1)
    def _():
        for k in others:
            relay_copy(k).wait_send()
            forward_copy(k).wait_send()

    @pl.when(s < last)
    def _():
        for m in range(micros):
            for part in range(2):
                hidden_copy(m, part).wait_send()

    @pl.when(s == last)
    def _():
        for m in range(micros):
            for to in range(sections):
                final_copy(m, to, 1).wait_send()
                if to != last:
                    final_copy(m, to, 0).wait_send()


def body(sections, windows, bands, tokens, regions, norm_gain, qkv_weight, out_weight, final_gain, dec_weight):
    micros, _, _, quad, width = tokens.shape
    inner = qkv_weight.shape[3]
    columns = dec_weight.shape[1]
    rows = bands * quad
    bf16 = jnp.bfloat16
    vmem = pl.BlockSpec(memory_space=pltpu.VMEM)
    hbm = pl.BlockSpec(memory_space=pl.ANY)
    dma = pltpu.SemaphoreType.DMA
    decoded = pl.pallas_call(
        functools.partial(kernel, sections, windows, bands),
        out_shape=jax.ShapeDtypeStruct((micros, quad, columns), bf16),
        in_specs=[vmem, vmem, vmem, hbm, hbm, vmem, hbm],
        out_specs=vmem,
        scratch_shapes=[
            pltpu.VMEM((micros, bands, quad, width), bf16),
            pltpu.VMEM((bands, quad, width), bf16),
            pltpu.VMEM((rows, width), bf16),
            pltpu.VMEM((3, rows, inner), bf16),
            pltpu.VMEM((3, width, inner), bf16),
            pltpu.VMEM((bands, inner, width), bf16),
            pltpu.VMEM((columns, width), bf16),
            pltpu.VMEM((rows, rows), jnp.float32),
            pltpu.VMEM((micros, bands, quad, inner), bf16),
            pltpu.VMEM((micros, bands, quad, inner), bf16),
            pltpu.VMEM((micros, quad, width), bf16),
            pltpu.VMEM((micros, quad, width), bf16),
            pltpu.VMEM((micros, quad, width), bf16),
            dma((micros, 3)), dma((micros, 3)),
            dma((micros, 3)), dma((micros, 3)),
            dma((micros, 2)), dma((micros, 2)),
            dma((micros, sections, 2)), dma((micros, 2)),
            dma((3,)), dma((3,)), dma((3,)),
            dma((3,)), dma((3,)),
            dma((3,)), dma((3,)),
            dma((6,)), dma((6,)),
            dma((3,)),
        ],
        compiler_params=pltpu.CompilerParams(
            collective_id=0, has_side_effects=True, vmem_limit_bytes=60 * 1024 * 1024
        ),
        name="relay",
    )(
        tokens[:, 0, 0],
        regions[0],
        norm_gain,
        jnp.transpose(qkv_weight[0], (1, 0, 2)),
        out_weight[0],
        final_gain[None],
        jnp.transpose(dec_weight),
    )
    return decoded[:, None, None]


def solution(mesh):
    sizes = mesh.shape
    return jax.shard_map(
        functools.partial(body, sizes["section"], sizes["win"], sizes["dp"]),
        mesh=mesh,
        in_specs=(
            P(None, "win", "dp", None, None),
            P("section", "win", None),
            P("section", None),
            P("section", None, None, "dp"),
            P("section", "dp", None),
            P(),
            P(None, "section"),
        ),
        out_specs=P(None, "win", "dp", None, "section"),
        check_vma=False,
    )
```

```python
import functools
import math

import jax
import jax.numpy as jnp
from jax import lax
from jax.experimental import pallas as pl
from jax.experimental.pallas import tpu as pltpu
from jax.sharding import PartitionSpec as P

HEAD_DIM = 64
MESH = pl.DeviceIdType.MESH
EXCLUDED = -1e30


def normalize(hidden, scales):
    values = hidden.astype(jnp.float32)
    center = values - jnp.mean(values, axis=-1, keepdims=True)
    spread = jnp.mean(center * center, axis=-1, keepdims=True)
    return (center * lax.rsqrt(spread + 1e-05) * scales).astype(jnp.bfloat16)


def kernel(
    sections, windows, bands,
    tokens, labels, gain, wqkv_hbm, wout_hbm, final_gain, wdec_hbm,
    decoded,
    full, relay_a, relay_b, ahead, normed, projected, wqkv, wout, wdec, bias, bstage, blend, hstage, fstage, final,
    ag_send, ag_recv, a2a_send, a2a_recv, hid_send, hid_recv, fin_send, fin_recv,
    rel_send, rel_recv, fwd_send, nx_send, nx_recv, nf_send, wz_send, wz_recv, wy_send, wy_recv, wc_send, wc_recv, load_sem,
):
    micros, quad, width = tokens.shape
    half = quad // 2
    last = sections - 1
    s = lax.axis_index("section")
    w = lax.axis_index("win")
    b = lax.axis_index("dp")
    before = lax.rem(w + windows - 1, windows)
    after = lax.rem(w + 1, windows)
    core_peer = w + 1 - 2 * lax.rem(w, 2)
    chip_peer = w + 2 - 4 * lax.rem(w // 2, 2)
    quarter = lax.rem(w, 4)
    group_rows = wout_hbm.shape[0]
    piece = group_rows // 4

    def band(k):
        return lax.rem(b + k, bands)

    def send(src, dst, send_sem, recv_sem, device):
        return pltpu.make_async_remote_copy(
            src_ref=src, dst_ref=dst, send_sem=send_sem, recv_sem=recv_sem,
            device_id=device, device_id_type=MESH,
        )

    def part_of(m, slot, part):
        return full.at[m, slot, pl.ds(half * part, half)]

    def ag_copy(m, k, part):
        slot = part_of(m, b, part)
        return send(slot, slot, ag_send.at[m, k - 1],
                    ag_recv.at[m, bands - k - 1, part], (s, w, band(k)))

    def ag_arrival(m, k, part):
        slot = part_of(m, band(k), part)
        return send(slot, slot, ag_send.at[m, k - 1], ag_recv.at[m, k - 1, part], (s, w, band(k)))

    def relay_copy(m, k):
        slot = (relay_b if m else relay_a).at[b]
        return send(slot, slot, rel_send.at[m, k - 1],
                    rel_recv.at[m, bands - k - 1], (s, w, band(k)))

    def relay_arrival(m, k):
        slot = (relay_b if m else relay_a).at[band(k)]
        return send(slot, slot, rel_send.at[m, k - 1], rel_recv.at[m, k - 1], (s, w, band(k)))

    def forward_copy(m, k, part):
        slot = relay_b.at[band(k), pl.ds(half * part, half)] if m else relay_a.at[band(k)]
        return send(slot, part_of(m, band(k), part), fwd_send.at[m + part if m else 0, k - 1],
                    ag_recv.at[m, k - 1, part], (0, w, b))

    def ahead_copy(m, k):
        return send(hstage.at[m, pl.ds(half, half)], ahead.at[m, b], nx_send.at[m, k - 1],
                    nx_recv.at[m, bands - k - 1], (s, w, band(k)))

    def ahead_arrival(m, k):
        slot = ahead.at[m, band(k)]
        return send(slot, slot, nx_send.at[m, k - 1], nx_recv.at[m, k - 1], (s, w, band(k)))

    def ahead_forward(m, k):
        return send(ahead.at[m, band(k)], part_of(m, band(k), 0), nf_send.at[m, k - 1],
                    ag_recv.at[m, k - 1, 0], (s + 1, w, b))

    def a2a_copy(m, k):
        return send(bstage.at[m, band(k)], blend.at[m, b], a2a_send.at[m, k - 1],
                    a2a_recv.at[m, bands - k - 1], (s, w, band(k)))

    def a2a_arrival(m, k):
        slot = blend.at[m, band(k)]
        return send(slot, slot, a2a_send.at[m, k - 1], a2a_recv.at[m, k - 1], (s, w, band(k)))

    def wz_copy(k):
        rows = pl.ds(pl.multiple_of(quarter * piece, piece), piece)
        return send(wout_hbm.at[rows], wout.at[b, rows], wz_send.at[k - 1],
                    wz_recv.at[bands - k - 1], (s, w, band(k)))

    def w_piece(k, owner):
        return wout.at[band(k), pl.ds(pl.multiple_of(lax.rem(owner, 4) * piece, piece), piece)]

    def wz_arrival(k):
        slot = w_piece(k, w)
        return send(slot, slot, wz_send.at[k - 1], wz_recv.at[k - 1], (s, w, band(k)))

    def wy_copy(k):
        slot = w_piece(k, w)
        return send(slot, slot, wy_send.at[k - 1], wy_recv.at[k - 1], (s, chip_peer, b))

    def wy_arrival(k):
        slot = w_piece(k, chip_peer)
        return send(slot, slot, wy_send.at[k - 1], wy_recv.at[k - 1], (s, chip_peer, b))

    def wc_copy(k, far):
        slot = w_piece(k, chip_peer if far else w)
        index = 3 * far + k - 1
        return send(slot, slot, wc_send.at[index], wc_recv.at[index], (s, core_peer, b))

    def wc_arrival(k, far):
        other = core_peer + 2 - 4 * lax.rem(core_peer // 2, 2)
        slot = w_piece(k, other if far else core_peer)
        index = 3 * far + k - 1
        return send(slot, slot, wc_send.at[index], wc_recv.at[index], (s, core_peer, b))

    def hidden_copy(m, part):
        rows_from = pl.ds(half * (1 - part), half)
        rows_to = pl.ds(half * part, half)
        return send(hstage.at[m, rows_from], full.at[m, b, rows_to], hid_send.at[m, part],
                    hid_recv.at[m, part], (s + 1, before if part else w, b))

    def hidden_arrival(m, part):
        slot = full.at[m, b, pl.ds(half * part, half)]
        return send(slot, slot, hid_send.at[m, part], hid_recv.at[m, part], (s, after, b))

    def final_copy(m, to, part):
        rows_from = pl.ds(half * (1 - part), half)
        rows_to = pl.ds(half * part, half)
        return send(fstage.at[m, rows_from], final.at[m, rows_to], fin_send.at[m, to, part],
                    fin_recv.at[m, part], (to, before if part else w, b))

    def final_arrival(m, part):
        slot = final.at[m, pl.ds(half * part, half)]
        return send(slot, slot, fin_send.at[m, 0, part], fin_recv.at[m, part], (s, after, b))

    others = range(1, bands)

    load_qkv = pltpu.make_async_copy(wqkv_hbm, wqkv, load_sem.at[0])
    load_out = pltpu.make_async_copy(wout_hbm, wout.at[b], load_sem.at[1])
    load_dec = pltpu.make_async_copy(wdec_hbm, wdec, load_sem.at[2])
    load_qkv.start()
    load_out.start()
    load_dec.start()

    barrier = pltpu.get_barrier_semaphore()
    partners = [(s, w, band(k)) for k in others]
    partners += [(s, core_peer, b), (s, chip_peer, b)]
    partners += [(lax.rem(s + k, sections), w, b) for k in range(1, sections)]
    for to in range(sections):
        partners += [(to, before, b), (to, after, b)]
    for device in partners:
        pl.semaphore_signal(barrier, inc=1, device_id=device, device_id_type=MESH)

    @pl.when(s == 0)
    def _():
        for m in range(micros):
            full[m, b] = tokens[m]

    @pl.when(s == 1)
    def _():
        relay_a[b] = tokens[0, half:]
        relay_b[b] = tokens[1]

    pl.semaphore_wait(barrier, len(partners))

    def start_gather(m):
        hidden_arrival(m, 1).wait_recv()
        for k in others:
            ag_copy(m, k, 1).start()
        hidden_arrival(m, 0).wait_recv()

    def start_weights():
        for k in others:
            wz_copy(k).start()

    def weights_over_chips():
        for k in others:
            wz_arrival(k).wait_recv()
            wy_copy(k).start()
            wc_copy(k, 0).start()

    def weights_over_cores():
        for k in others:
            wy_arrival(k).wait_recv()
            wc_copy(k, 1).start()

    def weights_all():
        for k in others:
            wc_arrival(k, 0).wait_recv()
            wc_arrival(k, 1).wait_recv()

    def normalize_band(m, slot):
        rows = pl.ds(pl.multiple_of(slot * quad, quad), quad)
        normed[rows, :] = normalize(full[m, slot], gain[...])

    def project(m):
        normalize_band(m, b)
        for k in others:
            ag_arrival(m, k, 0).wait_recv()
            ag_arrival(m, k, 1).wait_recv()
            normalize_band(m, band(k))
        if m == 0:
            load_qkv.wait()
        for c in range(3):
            projected[c] = jnp.dot(
                normed[...], wqkv[c], preferred_element_type=jnp.float32
            ).astype(jnp.bfloat16)

    def attend(m):
        inner = projected.shape[2]
        rows = projected.shape[1]
        lane = lax.broadcasted_iota(jnp.int32, (rows, 128), 1)
        for pair in range(inner // 128):
            columns = slice(128 * pair, 128 * pair + 128)
            queries = projected[0, :, columns]
            keys_all = projected[1, :, columns]
            values_all = projected[2, :, columns]
            results = []
            for side in range(128 // HEAD_DIM):
                mine = (lane // HEAD_DIM) == side
                query = jnp.where(mine, queries, jnp.zeros_like(queries))
                scores = lax.dot_general(
                    query, keys_all, (((1,), (1,)), ((), ())), preferred_element_type=jnp.float32
                ) * (1.0 / math.sqrt(HEAD_DIM)) + bias[...]
                largest = jnp.max(scores, axis=-1, keepdims=True)
                weights = jnp.exp(scores - largest)
                total = jnp.sum(weights, axis=-1, keepdims=True)
                product = jnp.dot(
                    weights.astype(jnp.bfloat16), values_all, preferred_element_type=jnp.float32
                )
                results.append(product / total)
            mixed = results[0]
            for side in range(1, 128 // HEAD_DIM):
                mixed = jnp.where((lane // HEAD_DIM) == side, results[side], mixed)
            mixed = mixed.astype(jnp.bfloat16)
            for place in range(bands):
                bstage[m, place, :, columns] = mixed[place * quad:(place + 1) * quad]
        for k in others:
            a2a_copy(m, k).start()
        blend[m, b] = bstage[m, b]

    def finish(m):
        for k in others:
            a2a_arrival(m, k).wait_recv()
        for start in range(0, width, 512):
            columns = slice(start, start + 512)
            total = full[m, b, :, columns].astype(jnp.float32)
            for group in range(bands):
                total += jnp.dot(
                    blend[m, group], wout[group, :, columns], preferred_element_type=jnp.float32
                )
            hstage[m, :, columns] = total.astype(jnp.bfloat16)

        @pl.when(s < last)
        def _():
            hidden_copy(m, 1).start()
            for k in others:
                ahead_copy(m, k).start()
            hidden_copy(m, 0).start()

        @pl.when(s == last)
        def _():
            fstage[m] = normalize(hstage[m], final_gain[...].reshape(1, width))
            for to in range(sections):
                final_copy(m, to, 1).start()
                if to != last:
                    final_copy(m, to, 0).start()
            final[m, :half] = fstage[m, half:]

    def decode(m):
        @pl.when(s < last)
        def _():
            final_arrival(m, 0).wait_recv()

        final_arrival(m, 1).wait_recv()
        decoded[m] = lax.dot_general(
            final[m], wdec[...], (((1,), (1,)), ((), ())), preferred_element_type=jnp.float32
        ).astype(jnp.bfloat16)

    row = labels[...].astype(jnp.float32)
    across = jnp.broadcast_to(row, bias.shape)

    @pl.when(s == 0)
    def _():
        start_weights()

    @pl.when(s == 1)
    def _():
        for k in others:
            relay_copy(0, k).start()

    bias[...] = jnp.where(across == across.T, 0.0, EXCLUDED)

    @pl.when(s == 1)
    def _():
        for k in others:
            relay_arrival(0, k).wait_recv()
            forward_copy(0, k, 1).start()
            if k == 1:
                for to in others:
                    relay_copy(1, to).start()
        for k in others:
            relay_arrival(1, k).wait_recv()
            forward_copy(1, k, 0).start()
            forward_copy(1, k, 1).start()

    @pl.when(s > 0)
    def _():
        start_weights()

    weights_over_chips()

    @pl.when(s == 0)
    def _():
        for k in others:
            ag_copy(0, k, 0).start()

    @pl.when(s > 0)
    def _():
        for m in range(micros):
            start_gather(m)

    project(0)
    attend(0)
    weights_over_cores()
    project(1)
    attend(1)
    load_out.wait()
    weights_all()
    finish(0)
    finish(1)

    @pl.when(s < last)
    def _():
        for m in range(micros):
            for k in others:
                ahead_arrival(m, k).wait_recv()
                ahead_forward(m, k).start()

    load_dec.wait()
    decode(0)
    decode(1)

    for m in range(micros):
        for k in others:
            a2a_copy(m, k).wait_send()
    for k in others:
        wz_copy(k).wait_send()
        wy_copy(k).wait_send()
        wc_copy(k, 0).wait_send()
        wc_copy(k, 1).wait_send()

    @pl.when(s == 0)
    def _():
        for k in others:
            ag_copy(0, k, 0).wait_send()

    @pl.when(s > 0)
    def _():
        for m in range(micros):
            for k in others:
                ag_copy(m, k, 1).wait_send()

    @pl.when(s == 1)
    def _():
        for k in others:
            relay_copy(0, k).wait_send()
            relay_copy(1, k).wait_send()
            forward_copy(0, k, 1).wait_send()
            forward_copy(1, k, 0).wait_send()
            forward_copy(1, k, 1).wait_send()

    @pl.when(s < last)
    def _():
        for m in range(micros):
            for part in range(2):
                hidden_copy(m, part).wait_send()
            for k in others:
                ahead_copy(m, k).wait_send()
                ahead_forward(m, k).wait_send()

    @pl.when(s == last)
    def _():
        for m in range(micros):
            for to in range(sections):
                final_copy(m, to, 1).wait_send()
                if to != last:
                    final_copy(m, to, 0).wait_send()


def body(sections, windows, bands, tokens, regions, norm_gain, qkv_weight, out_weight, final_gain, dec_weight):
    micros, _, _, quad, width = tokens.shape
    inner = qkv_weight.shape[3]
    columns = dec_weight.shape[1]
    rows = bands * quad
    bf16 = jnp.bfloat16
    vmem = pl.BlockSpec(memory_space=pltpu.VMEM)
    hbm = pl.BlockSpec(memory_space=pl.ANY)
    dma = pltpu.SemaphoreType.DMA
    decoded = pl.pallas_call(
        functools.partial(kernel, sections, windows, bands),
        out_shape=jax.ShapeDtypeStruct((micros, quad, columns), bf16),
        in_specs=[vmem, vmem, vmem, hbm, hbm, vmem, hbm],
        out_specs=vmem,
        scratch_shapes=[
            pltpu.VMEM((micros, bands, quad, width), bf16),
            pltpu.VMEM((bands, quad // 2, width), bf16),
            pltpu.VMEM((bands, quad, width), bf16),
            pltpu.VMEM((micros, bands, quad // 2, width), bf16),
            pltpu.VMEM((rows, width), bf16),
            pltpu.VMEM((3, rows, inner), bf16),
            pltpu.VMEM((3, width, inner), bf16),
            pltpu.VMEM((bands, inner, width), bf16),
            pltpu.VMEM((columns, width), bf16),
            pltpu.VMEM((rows, rows), jnp.float32),
            pltpu.VMEM((micros, bands, quad, inner), bf16),
            pltpu.VMEM((micros, bands, quad, inner), bf16),
            pltpu.VMEM((micros, quad, width), bf16),
            pltpu.VMEM((micros, quad, width), bf16),
            pltpu.VMEM((micros, quad, width), bf16),
            dma((micros, 3)), dma((micros, 3, 2)),
            dma((micros, 3)), dma((micros, 3)),
            dma((micros, 2)), dma((micros, 2)),
            dma((micros, sections, 2)), dma((micros, 2)),
            dma((2, 3)), dma((2, 3)), dma((3, 3)),
            dma((micros, 3)), dma((micros, 3)), dma((micros, 3)),
            dma((3,)), dma((3,)),
            dma((3,)), dma((3,)),
            dma((6,)), dma((6,)),
            dma((3,)),
        ],
        compiler_params=pltpu.CompilerParams(
            collective_id=0, has_side_effects=True, vmem_limit_bytes=60 * 1024 * 1024
        ),
        name="relay",
    )(
        tokens[:, 0, 0],
        regions[0],
        norm_gain,
        jnp.transpose(qkv_weight[0], (1, 0, 2)),
        out_weight[0],
        final_gain,
        jnp.transpose(dec_weight),
    )
    return decoded[:, None, None]


def solution(mesh):
    sizes = mesh.shape
    return jax.shard_map(
        functools.partial(body, sizes["section"], sizes["win"], sizes["dp"]),
        mesh=mesh,
        in_specs=(
            P(None, "win", "dp", None, None),
            P("section", "win", None),
            P("section", None),
            P("section", None, None, "dp"),
            P("section", "dp", None),
            P(),
            P(None, "section"),
        ),
        out_specs=P(None, "win", "dp", None, "section"),
        check_vma=False,
    )
```

```python
import functools
import math

import jax
import jax.numpy as jnp
from jax import lax
from jax.experimental import pallas as pl
from jax.experimental.pallas import tpu as pltpu
from jax.sharding import PartitionSpec as P

HEAD_DIM = 64
MESH = pl.DeviceIdType.MESH
EXCLUDED = -1e30


def normalize(hidden, scales):
    values = hidden.astype(jnp.float32)
    center = values - jnp.mean(values, axis=-1, keepdims=True)
    spread = jnp.mean(center * center, axis=-1, keepdims=True)
    return (center * lax.rsqrt(spread + 1e-05) * scales).astype(jnp.bfloat16)


def kernel(
    sections, windows, bands,
    tokens, labels, gain, wqkv_hbm, wout_hbm, final_gain, wdec_hbm,
    decoded,
    full, relay_a, relay_b, ahead, normed, projected, wqkv, wout, wdec, bias, bstage, blend, hstage, fstage, final,
    ag_send, ag_recv, a2a_send, a2a_recv, hid_send, hid_recv, fin_send, fin_recv,
    chain_send, chain_recv, fwd_send, nx_send, nx_recv, nf_send, wy_send, wy_recv, wc_send, wc_recv, load_sem,
):
    micros, quad, width = tokens.shape
    half = quad // 2
    last = sections - 1
    s = lax.axis_index("section")
    w = lax.axis_index("win")
    b = lax.axis_index("dp")
    before = lax.rem(w + windows - 1, windows)
    after = lax.rem(w + 1, windows)
    core_peer = w + 1 - 2 * lax.rem(w, 2)
    chip_peer = w + 2 - 4 * lax.rem(w // 2, 2)
    quarter = lax.rem(w, 4)
    group_rows = wout_hbm.shape[0]
    piece = group_rows // 8

    def band(k):
        return lax.rem(b + k, bands)

    def send(src, dst, send_sem, recv_sem, device):
        return pltpu.make_async_remote_copy(
            src_ref=src, dst_ref=dst, send_sem=send_sem, recv_sem=recv_sem,
            device_id=device, device_id_type=MESH,
        )

    def part_of(m, slot, part):
        return full.at[m, slot, pl.ds(half * part, half)]

    def ag_copy(m, k, part):
        slot = part_of(m, b, part)
        return send(slot, slot, ag_send.at[m, k - 1],
                    ag_recv.at[m, bands - k - 1, part], (s, w, band(k)))

    def ag_arrival(m, k, part):
        slot = part_of(m, band(k), part)
        return send(slot, slot, ag_send.at[m, k - 1], ag_recv.at[m, k - 1, part], (s, w, band(k)))

    class Chain:
        def __init__(self, index, slot, arrived):
            self.index, self.slot, self.arrived = index, slot, arrived

        def copy(self, way, distance, source):
            slot = self.slot(source)
            step = -1 if way else 1
            return send(slot, slot, chain_send.at[self.index, way, distance],
                        chain_recv.at[self.index, way, distance], (s, w, b + step))

        def each(self, distance, do):
            @pl.when((b >= distance) & (b < bands - 1))
            def _():
                do(self.copy(0, distance, b - distance))

            @pl.when((b + distance < bands) & (b > 0))
            def _():
                do(self.copy(1, distance, b + distance))

        def start(self):
            self.each(0, lambda copy: copy.start())

        def serve(self, distance):
            @pl.when(b >= distance)
            def _():
                self.copy(0, distance - 1, b - distance).wait_recv()

                if distance < bands - 1:
                    @pl.when(b < bands - 1)
                    def _():
                        self.copy(0, distance, b - distance).start()

                self.arrived(bands - distance)

            @pl.when(b + distance < bands)
            def _():
                self.copy(1, distance - 1, b + distance).wait_recv()

                if distance < bands - 1:
                    @pl.when(b > 0)
                    def _():
                        self.copy(1, distance, b + distance).start()

                self.arrived(distance)

        def drain(self):
            for distance in range(bands - 1):
                self.each(distance, lambda copy: copy.wait_send())

    def forward_copy(m, k, part):
        slot = relay_b.at[band(k), pl.ds(half * part, half)] if m else relay_a.at[band(k)]
        return send(slot, part_of(m, band(k), part), fwd_send.at[m + part if m else 0, k - 1],
                    ag_recv.at[m, k - 1, part], (0, w, b))

    def ahead_copy(m, k):
        return send(hstage.at[m, pl.ds(half, half)], ahead.at[m, b], nx_send.at[m, k - 1],
                    nx_recv.at[m, bands - k - 1], (s, w, band(k)))

    def ahead_arrival(m, k):
        slot = ahead.at[m, band(k)]
        return send(slot, slot, nx_send.at[m, k - 1], nx_recv.at[m, k - 1], (s, w, band(k)))

    def ahead_forward(m, k):
        return send(ahead.at[m, band(k)], part_of(m, band(k), 0), nf_send.at[m, k - 1],
                    ag_recv.at[m, k - 1, 0], (s + 1, w, b))

    def a2a_copy(m, k):
        return send(bstage.at[m, band(k)], blend.at[m, b], a2a_send.at[m, k - 1],
                    a2a_recv.at[m, bands - k - 1], (s, w, band(k)))

    def a2a_arrival(m, k):
        slot = blend.at[m, band(k)]
        return send(slot, slot, a2a_send.at[m, k - 1], a2a_recv.at[m, k - 1], (s, w, band(k)))

    def w_piece(slot, owner, chunk):
        start = (lax.rem(owner, 4) * 2 + chunk) * piece
        return wout.at[slot, pl.ds(pl.multiple_of(start, piece), piece)]

    def wy_copy(k, chunk):
        slot = w_piece(band(k), w, chunk)
        return send(slot, slot, wy_send.at[chunk, k - 1], wy_recv.at[chunk, k - 1], (s, chip_peer, b))

    def wy_arrival(k, chunk):
        slot = w_piece(band(k), chip_peer, chunk)
        return send(slot, slot, wy_send.at[chunk, k - 1], wy_recv.at[chunk, k - 1], (s, chip_peer, b))

    def wc_copy(k, far, chunk):
        slot = w_piece(band(k), chip_peer if far else w, chunk)
        index = 3 * far + k - 1
        return send(slot, slot, wc_send.at[chunk, index], wc_recv.at[chunk, index], (s, core_peer, b))

    def wc_arrival(k, far, chunk):
        other = core_peer + 2 - 4 * lax.rem(core_peer // 2, 2)
        slot = w_piece(band(k), other if far else core_peer, chunk)
        index = 3 * far + k - 1
        return send(slot, slot, wc_send.at[chunk, index], wc_recv.at[chunk, index], (s, core_peer, b))

    def hidden_copy(m, part):
        rows_from = pl.ds(half * (1 - part), half)
        rows_to = pl.ds(half * part, half)
        return send(hstage.at[m, rows_from], full.at[m, b, rows_to], hid_send.at[m, part],
                    hid_recv.at[m, part], (s + 1, before if part else w, b))

    def hidden_arrival(m, part):
        slot = full.at[m, b, pl.ds(half * part, half)]
        return send(slot, slot, hid_send.at[m, part], hid_recv.at[m, part], (s, after, b))

    def final_copy(m, to, part):
        rows_from = pl.ds(half * (1 - part), half)
        rows_to = pl.ds(half * part, half)
        return send(fstage.at[m, rows_from], final.at[m, rows_to], fin_send.at[m, to, part],
                    fin_recv.at[m, part], (to, before if part else w, b))

    def final_arrival(m, part):
        slot = final.at[m, pl.ds(half * part, half)]
        return send(slot, slot, fin_send.at[m, 0, part], fin_recv.at[m, part], (s, after, b))

    others = range(1, bands)
    chunks = range(2)

    def weights_arrived(chunk):
        def arrived(k):
            wy_copy(k, chunk).start()
            wc_copy(k, 0, chunk).start()
        return arrived

    def relayed(m, part):
        return lambda k: forward_copy(m, k, part).start()

    first_half = Chain(0, lambda slot: part_of(0, slot, 0), lambda k: None)
    relay_first = Chain(0, lambda slot: relay_a.at[slot], relayed(0, 1))
    weight_chains = [
        Chain(1 + c, lambda slot, c=c: w_piece(slot, w, c), weights_arrived(c)) for c in chunks
    ]
    relay_second = [
        Chain(3 + c, lambda slot, c=c: relay_b.at[slot, pl.ds(half * c, half)], relayed(1, c))
        for c in chunks
    ]

    load_qkv = pltpu.make_async_copy(wqkv_hbm, wqkv, load_sem.at[0])
    load_out = pltpu.make_async_copy(wout_hbm, wout.at[b], load_sem.at[1])
    load_dec = pltpu.make_async_copy(wdec_hbm, wdec, load_sem.at[2])
    load_qkv.start()
    load_out.start()
    load_dec.start()

    barrier = pltpu.get_barrier_semaphore()
    partners = [(s, w, band(k)) for k in others]
    partners += [(s, core_peer, b), (s, chip_peer, b)]
    partners += [(lax.rem(s + k, sections), w, b) for k in range(1, sections)]
    for to in range(sections):
        partners += [(to, before, b), (to, after, b)]
    for device in partners:
        pl.semaphore_signal(barrier, inc=1, device_id=device, device_id_type=MESH)

    @pl.when(s == 0)
    def _():
        for m in range(micros):
            full[m, b] = tokens[m]

    @pl.when(s == 1)
    def _():
        relay_a[b] = tokens[0, half:]
        relay_b[b] = tokens[1]

    pl.semaphore_wait(barrier, len(partners))

    def start_gather(m):
        hidden_arrival(m, 1).wait_recv()
        for k in others:
            ag_copy(m, k, 1).start()
        hidden_arrival(m, 0).wait_recv()

    def weights_over_cores():
        for k in others:
            for chunk in chunks:
                wy_arrival(k, chunk).wait_recv()
                wc_copy(k, 1, chunk).start()

    def weights_all():
        for k in others:
            for chunk in chunks:
                wc_arrival(k, 0, chunk).wait_recv()
                wc_arrival(k, 1, chunk).wait_recv()

    def normalize_band(m, slot):
        rows = pl.ds(pl.multiple_of(slot * quad, quad), quad)
        normed[rows, :] = normalize(full[m, slot], gain[...])

    def project(m):
        normalize_band(m, b)
        for k in others:
            if m == 0:
                @pl.when(s > 0)
                def _():
                    ag_arrival(m, k, 0).wait_recv()
            else:
                ag_arrival(m, k, 0).wait_recv()
            ag_arrival(m, k, 1).wait_recv()
            normalize_band(m, band(k))
        if m == 0:
            load_qkv.wait()
        for c in range(3):
            projected[c] = jnp.dot(
                normed[...], wqkv[c], preferred_element_type=jnp.float32
            ).astype(jnp.bfloat16)

    def attend(m):
        inner = projected.shape[2]
        rows = projected.shape[1]
        lane = lax.broadcasted_iota(jnp.int32, (rows, 128), 1)
        for pair in range(inner // 128):
            columns = slice(128 * pair, 128 * pair + 128)
            queries = projected[0, :, columns]
            keys_all = projected[1, :, columns]
            values_all = projected[2, :, columns]
            results = []
            for side in range(128 // HEAD_DIM):
                mine = (lane // HEAD_DIM) == side
                query = jnp.where(mine, queries, jnp.zeros_like(queries))
                scores = lax.dot_general(
                    query, keys_all, (((1,), (1,)), ((), ())), preferred_element_type=jnp.float32
                ) * (1.0 / math.sqrt(HEAD_DIM)) + bias[...]
                largest = jnp.max(scores, axis=-1, keepdims=True)
                weights = jnp.exp(scores - largest)
                total = jnp.sum(weights, axis=-1, keepdims=True)
                product = jnp.dot(
                    weights.astype(jnp.bfloat16), values_all, preferred_element_type=jnp.float32
                )
                results.append(product / total)
            mixed = results[0]
            for side in range(1, 128 // HEAD_DIM):
                mixed = jnp.where((lane // HEAD_DIM) == side, results[side], mixed)
            mixed = mixed.astype(jnp.bfloat16)
            for place in range(bands):
                bstage[m, place, :, columns] = mixed[place * quad:(place + 1) * quad]
        for k in others:
            a2a_copy(m, k).start()
        blend[m, b] = bstage[m, b]

    def finish(m):
        for k in others:
            a2a_arrival(m, k).wait_recv()
        for start in range(0, width, 512):
            columns = slice(start, start + 512)
            total = full[m, b, :, columns].astype(jnp.float32)
            for group in range(bands):
                total += jnp.dot(
                    blend[m, group], wout[group, :, columns], preferred_element_type=jnp.float32
                )
            hstage[m, :, columns] = total.astype(jnp.bfloat16)

        @pl.when(s < last)
        def _():
            hidden_copy(m, 1).start()
            for k in others:
                ahead_copy(m, k).start()
            hidden_copy(m, 0).start()

        @pl.when(s == last)
        def _():
            fstage[m] = normalize(hstage[m], final_gain[...].reshape(1, width))
            for to in range(sections):
                final_copy(m, to, 1).start()
                if to != last:
                    final_copy(m, to, 0).start()
            final[m, :half] = fstage[m, half:]

    def decode(m):
        @pl.when(s < last)
        def _():
            final_arrival(m, 0).wait_recv()

        final_arrival(m, 1).wait_recv()
        decoded[m] = lax.dot_general(
            final[m], wdec[...], (((1,), (1,)), ((), ())), preferred_element_type=jnp.float32
        ).astype(jnp.bfloat16)

    row = labels[...].astype(jnp.float32)
    across = jnp.broadcast_to(row, bias.shape)

    load_out.wait()

    @pl.when(s == 0)
    def _():
        for chain in weight_chains:
            chain.start()

    @pl.when(s == 1)
    def _():
        relay_first.start()

    bias[...] = jnp.where(across == across.T, 0.0, EXCLUDED)

    @pl.when(s == 1)
    def _():
        relay_first.serve(1)
        relay_second[0].start()
        relay_first.serve(2)
        relay_second[1].start()
        relay_first.serve(3)
        for distance in others:
            for chain in relay_second:
                chain.serve(distance)
            if distance == 2:
                for chain in weight_chains:
                    chain.start()

    @pl.when(s > 1)
    def _():
        for chain in weight_chains:
            chain.start()

    for distance in others:
        for chain in weight_chains:
            chain.serve(distance)
        if distance == 2:
            @pl.when(s == 0)
            def _():
                first_half.start()

    @pl.when(s == 0)
    def _():
        for distance in others:
            first_half.serve(distance)
        weights_over_cores()

    @pl.when(s > 0)
    def _():
        for m in range(micros):
            start_gather(m)
        weights_over_cores()

    def hand_over(m):
        @pl.when(s < last)
        def _():
            for k in others:
                ahead_arrival(m, k).wait_recv()
                ahead_forward(m, k).start()

    project(0)
    attend(0)
    weights_all()
    project(1)

    @pl.when(s < last)
    def _():
        finish(0)

    attend(1)

    @pl.when(s == last)
    def _():
        finish(0)

    hand_over(0)
    finish(1)
    hand_over(1)
    load_dec.wait()
    decode(0)
    decode(1)

    for m in range(micros):
        for k in others:
            a2a_copy(m, k).wait_send()
    for chain in weight_chains:
        chain.drain()
    for k in others:
        for chunk in chunks:
            wy_copy(k, chunk).wait_send()
            wc_copy(k, 0, chunk).wait_send()
            wc_copy(k, 1, chunk).wait_send()

    @pl.when(s == 0)
    def _():
        first_half.drain()

    @pl.when(s > 0)
    def _():
        for m in range(micros):
            for k in others:
                ag_copy(m, k, 1).wait_send()

    @pl.when(s == 1)
    def _():
        for chain in [relay_first, *relay_second]:
            chain.drain()
        for k in others:
            forward_copy(0, k, 1).wait_send()
            forward_copy(1, k, 0).wait_send()
            forward_copy(1, k, 1).wait_send()

    @pl.when(s < last)
    def _():
        for m in range(micros):
            for part in range(2):
                hidden_copy(m, part).wait_send()
            for k in others:
                ahead_copy(m, k).wait_send()
                ahead_forward(m, k).wait_send()

    @pl.when(s == last)
    def _():
        for m in range(micros):
            for to in range(sections):
                final_copy(m, to, 1).wait_send()
                if to != last:
                    final_copy(m, to, 0).wait_send()


def body(sections, windows, bands, tokens, regions, norm_gain, qkv_weight, out_weight, final_gain, dec_weight):
    micros, _, _, quad, width = tokens.shape
    inner = qkv_weight.shape[3]
    columns = dec_weight.shape[1]
    rows = bands * quad
    bf16 = jnp.bfloat16
    vmem = pl.BlockSpec(memory_space=pltpu.VMEM)
    hbm = pl.BlockSpec(memory_space=pl.ANY)
    dma = pltpu.SemaphoreType.DMA
    decoded = pl.pallas_call(
        functools.partial(kernel, sections, windows, bands),
        out_shape=jax.ShapeDtypeStruct((micros, quad, columns), bf16),
        in_specs=[vmem, vmem, vmem, hbm, hbm, vmem, hbm],
        out_specs=vmem,
        scratch_shapes=[
            pltpu.VMEM((micros, bands, quad, width), bf16),
            pltpu.VMEM((bands, quad // 2, width), bf16),
            pltpu.VMEM((bands, quad, width), bf16),
            pltpu.VMEM((micros, bands, quad // 2, width), bf16),
            pltpu.VMEM((rows, width), bf16),
            pltpu.VMEM((3, rows, inner), bf16),
            pltpu.VMEM((3, width, inner), bf16),
            pltpu.VMEM((bands, inner, width), bf16),
            pltpu.VMEM((columns, width), bf16),
            pltpu.VMEM((rows, rows), jnp.float32),
            pltpu.VMEM((micros, bands, quad, inner), bf16),
            pltpu.VMEM((micros, bands, quad, inner), bf16),
            pltpu.VMEM((micros, quad, width), bf16),
            pltpu.VMEM((micros, quad, width), bf16),
            pltpu.VMEM((micros, quad, width), bf16),
            dma((micros, 3)), dma((micros, 3, 2)),
            dma((micros, 3)), dma((micros, 3)),
            dma((micros, 2)), dma((micros, 2)),
            dma((micros, sections, 2)), dma((micros, 2)),
            dma((5, 2, 3)), dma((5, 2, 3)), dma((3, 3)),
            dma((micros, 3)), dma((micros, 3)), dma((micros, 3)),
            dma((2, 3)), dma((2, 3)),
            dma((2, 6)), dma((2, 6)),
            dma((3,)),
        ],
        compiler_params=pltpu.CompilerParams(
            collective_id=0, has_side_effects=True, vmem_limit_bytes=60 * 1024 * 1024
        ),
        name="relay",
    )(
        tokens[:, 0, 0],
        regions[0],
        norm_gain,
        jnp.transpose(qkv_weight[0], (1, 0, 2)),
        out_weight[0],
        final_gain,
        jnp.transpose(dec_weight),
    )
    return decoded[:, None, None]


def solution(mesh):
    sizes = mesh.shape
    return jax.shard_map(
        functools.partial(body, sizes["section"], sizes["win"], sizes["dp"]),
        mesh=mesh,
        in_specs=(
            P(None, "win", "dp", None, None),
            P("section", "win", None),
            P("section", None),
            P("section", None, None, "dp"),
            P("section", "dp", None),
            P(),
            P(None, "section"),
        ),
        out_specs=P(None, "win", "dp", None, "section"),
        check_vma=False,
    )
```

```python
import functools
import math

import jax
import jax.numpy as jnp
from jax import lax
from jax.experimental import pallas as pl
from jax.experimental.pallas import tpu as pltpu
from jax.sharding import PartitionSpec as P

HEAD_DIM = 64
MESH = pl.DeviceIdType.MESH
EXCLUDED = -1e30


def normalize(hidden, scales):
    values = hidden.astype(jnp.float32)
    center = values - jnp.mean(values, axis=-1, keepdims=True)
    spread = jnp.mean(center * center, axis=-1, keepdims=True)
    return (center * lax.rsqrt(spread + 1e-05) * scales).astype(jnp.bfloat16)


def kernel(
    sections, windows, bands,
    tokens, labels, gain, wqkv_hbm, wout_hbm, final_gain, wdec_hbm,
    decoded,
    full, relay_a, relay_b, ahead, normed, projected, wqkv, wout, wdec, bias, bstage, blend, hstage, fstage, final,
    ag_send, ag_recv, a2a_send, a2a_recv, hid_send, hid_recv, fin_send, fin_recv,
    chain_send, chain_recv, fwd_send, nx_send, nx_recv, nf_send, wy_send, wy_recv, wc_send, wc_recv, load_sem,
):
    micros, quad, width = tokens.shape
    half = quad // 2
    last = sections - 1
    s = lax.axis_index("section")
    w = lax.axis_index("win")
    b = lax.axis_index("dp")
    before = lax.rem(w + windows - 1, windows)
    after = lax.rem(w + 1, windows)
    core_peer = w + 1 - 2 * lax.rem(w, 2)
    chip_peer = w + 2 - 4 * lax.rem(w // 2, 2)
    quarter = lax.rem(w, 4)
    group_rows = wout_hbm.shape[0]
    piece = group_rows // 8

    def band(k):
        return lax.rem(b + k, bands)

    def send(src, dst, send_sem, recv_sem, device):
        return pltpu.make_async_remote_copy(
            src_ref=src, dst_ref=dst, send_sem=send_sem, recv_sem=recv_sem,
            device_id=device, device_id_type=MESH,
        )

    def part_of(m, slot, part):
        return full.at[m, slot, pl.ds(half * part, half)]

    def ag_copy(m, k, part):
        slot = part_of(m, b, part)
        return send(slot, slot, ag_send.at[m, k - 1],
                    ag_recv.at[m, bands - k - 1, part], (s, w, band(k)))

    def ag_arrival(m, k, part):
        slot = part_of(m, band(k), part)
        return send(slot, slot, ag_send.at[m, k - 1], ag_recv.at[m, k - 1, part], (s, w, band(k)))

    class Chain:
        def __init__(self, index, slot, arrived):
            self.index, self.slot, self.arrived = index, slot, arrived

        def copy(self, way, distance, source):
            slot = self.slot(source)
            step = -1 if way else 1
            return send(slot, slot, chain_send.at[self.index, way, distance],
                        chain_recv.at[self.index, way, distance], (s, w, b + step))

        def each(self, distance, do):
            @pl.when((b >= distance) & (b < bands - 1))
            def _():
                do(self.copy(0, distance, b - distance))

            @pl.when((b + distance < bands) & (b > 0))
            def _():
                do(self.copy(1, distance, b + distance))

        def start(self):
            self.each(0, lambda copy: copy.start())

        def serve(self, distance):
            @pl.when(b >= distance)
            def _():
                self.copy(0, distance - 1, b - distance).wait_recv()

                if distance < bands - 1:
                    @pl.when(b < bands - 1)
                    def _():
                        self.copy(0, distance, b - distance).start()

                self.arrived(bands - distance)

            @pl.when(b + distance < bands)
            def _():
                self.copy(1, distance - 1, b + distance).wait_recv()

                if distance < bands - 1:
                    @pl.when(b > 0)
                    def _():
                        self.copy(1, distance, b + distance).start()

                self.arrived(distance)

        def drain(self):
            for distance in range(bands - 1):
                self.each(distance, lambda copy: copy.wait_send())

    def forward_copy(m, k, part):
        slot = relay_b.at[band(k), pl.ds(half * part, half)] if m else relay_a.at[band(k)]
        return send(slot, part_of(m, band(k), part), fwd_send.at[m + part if m else 0, k - 1],
                    ag_recv.at[m, k - 1, part], (0, w, b))

    def ahead_copy(m, k):
        return send(hstage.at[m, pl.ds(half, half)], ahead.at[m, b], nx_send.at[m, k - 1],
                    nx_recv.at[m, bands - k - 1], (s, w, band(k)))

    def ahead_arrival(m, k):
        slot = ahead.at[m, band(k)]
        return send(slot, slot, nx_send.at[m, k - 1], nx_recv.at[m, k - 1], (s, w, band(k)))

    def ahead_forward(m, k):
        return send(ahead.at[m, band(k)], part_of(m, band(k), 0), nf_send.at[m, k - 1],
                    ag_recv.at[m, k - 1, 0], (s + 1, w, b))

    def a2a_copy(m, k):
        return send(bstage.at[m, band(k)], blend.at[m, b], a2a_send.at[m, k - 1],
                    a2a_recv.at[m, bands - k - 1], (s, w, band(k)))

    def a2a_arrival(m, k):
        slot = blend.at[m, band(k)]
        return send(slot, slot, a2a_send.at[m, k - 1], a2a_recv.at[m, k - 1], (s, w, band(k)))

    def w_piece(slot, owner, chunk):
        start = (lax.rem(owner, 4) * 2 + chunk) * piece
        return wout.at[slot, pl.ds(pl.multiple_of(start, piece), piece)]

    def wy_copy(k, chunk):
        slot = w_piece(band(k), w, chunk)
        return send(slot, slot, wy_send.at[chunk, k - 1], wy_recv.at[chunk, k - 1], (s, chip_peer, b))

    def wy_arrival(k, chunk):
        slot = w_piece(band(k), chip_peer, chunk)
        return send(slot, slot, wy_send.at[chunk, k - 1], wy_recv.at[chunk, k - 1], (s, chip_peer, b))

    def wc_copy(k, far, chunk):
        slot = w_piece(band(k), chip_peer if far else w, chunk)
        index = 3 * far + k - 1
        return send(slot, slot, wc_send.at[chunk, index], wc_recv.at[chunk, index], (s, core_peer, b))

    def wc_arrival(k, far, chunk):
        other = core_peer + 2 - 4 * lax.rem(core_peer // 2, 2)
        slot = w_piece(band(k), other if far else core_peer, chunk)
        index = 3 * far + k - 1
        return send(slot, slot, wc_send.at[chunk, index], wc_recv.at[chunk, index], (s, core_peer, b))

    def hidden_copy(m, part):
        rows_from = pl.ds(half * (1 - part), half)
        rows_to = pl.ds(half * part, half)
        return send(hstage.at[m, rows_from], full.at[m, b, rows_to], hid_send.at[m, part],
                    hid_recv.at[m, part], (s + 1, before if part else w, b))

    def hidden_arrival(m, part):
        slot = full.at[m, b, pl.ds(half * part, half)]
        return send(slot, slot, hid_send.at[m, part], hid_recv.at[m, part], (s, after, b))

    def final_copy(m, to, part):
        rows_from = pl.ds(half * (1 - part), half)
        rows_to = pl.ds(half * part, half)
        return send(fstage.at[m, rows_from], final.at[m, rows_to], fin_send.at[m, to, part],
                    fin_recv.at[m, part], (to, before if part else w, b))

    def final_arrival(m, part):
        slot = final.at[m, pl.ds(half * part, half)]
        return send(slot, slot, fin_send.at[m, 0, part], fin_recv.at[m, part], (s, after, b))

    others = range(1, bands)
    chunks = range(2)

    def weights_arrived(chunk):
        def arrived(k):
            wy_copy(k, chunk).start()
            wc_copy(k, 0, chunk).start()
        return arrived

    def relayed(m, part):
        return lambda k: forward_copy(m, k, part).start()

    first_half = Chain(0, lambda slot: part_of(0, slot, 0), lambda k: None)
    relay_first = Chain(0, lambda slot: relay_a.at[slot], relayed(0, 1))
    weight_chains = [
        Chain(1 + c, lambda slot, c=c: w_piece(slot, w, c), weights_arrived(c)) for c in chunks
    ]
    relay_second = [
        Chain(3 + c, lambda slot, c=c: relay_b.at[slot, pl.ds(half * c, half)], relayed(1, c))
        for c in chunks
    ]

    load_qkv = pltpu.make_async_copy(wqkv_hbm, wqkv, load_sem.at[0])
    load_out = pltpu.make_async_copy(wout_hbm, wout.at[b], load_sem.at[1])
    load_dec = pltpu.make_async_copy(wdec_hbm, wdec, load_sem.at[2])
    load_qkv.start()
    load_out.start()
    load_dec.start()

    barrier = pltpu.get_barrier_semaphore()
    partners = [(s, w, band(k)) for k in others]
    partners += [(s, core_peer, b), (s, chip_peer, b)]
    partners += [(lax.rem(s + k, sections), w, b) for k in range(1, sections)]
    for to in range(sections):
        partners += [(to, before, b), (to, after, b)]
    for device in partners:
        pl.semaphore_signal(barrier, inc=1, device_id=device, device_id_type=MESH)

    @pl.when(s == 0)
    def _():
        for m in range(micros):
            full[m, b] = tokens[m]

    @pl.when(s == 1)
    def _():
        relay_a[b] = tokens[0, half:]
        relay_b[b] = tokens[1]

    pl.semaphore_wait(barrier, len(partners))

    def start_gather(m):
        hidden_arrival(m, 1).wait_recv()
        for k in others:
            ag_copy(m, k, 1).start()
        hidden_arrival(m, 0).wait_recv()

    def weights_over_cores():
        for k in others:
            for chunk in chunks:
                wy_arrival(k, chunk).wait_recv()
                wc_copy(k, 1, chunk).start()

    def weights_all():
        for k in others:
            for chunk in chunks:
                wc_arrival(k, 0, chunk).wait_recv()
                wc_arrival(k, 1, chunk).wait_recv()

    def normalize_band(m, slot):
        rows = pl.ds(pl.multiple_of(slot * quad, quad), quad)
        normed[rows, :] = normalize(full[m, slot], gain[...])

    def project(m):
        normalize_band(m, b)
        for k in others:
            if m == 0:
                @pl.when(s > 0)
                def _():
                    ag_arrival(m, k, 0).wait_recv()
            else:
                ag_arrival(m, k, 0).wait_recv()
            ag_arrival(m, k, 1).wait_recv()
            normalize_band(m, band(k))
        if m == 0:
            load_qkv.wait()
        for c in range(3):
            projected[c] = jnp.dot(
                normed[...], wqkv[c], preferred_element_type=jnp.float32
            ).astype(jnp.bfloat16)

    def attend(m):
        inner = projected.shape[2]
        rows = projected.shape[1]
        lane = lax.broadcasted_iota(jnp.int32, (rows, 128), 1)
        for pair in range(inner // 128):
            columns = slice(128 * pair, 128 * pair + 128)
            queries = projected[0, :, columns]
            keys_all = projected[1, :, columns]
            values_all = projected[2, :, columns]
            results = []
            for side in range(128 // HEAD_DIM):
                mine = (lane // HEAD_DIM) == side
                query = jnp.where(mine, queries, jnp.zeros_like(queries))
                scores = lax.dot_general(
                    query, keys_all, (((1,), (1,)), ((), ())), preferred_element_type=jnp.float32
                ) * (1.0 / math.sqrt(HEAD_DIM)) + bias[...]
                largest = jnp.max(scores, axis=-1, keepdims=True)
                weights = jnp.exp(scores - largest)
                total = jnp.sum(weights, axis=-1, keepdims=True)
                product = jnp.dot(
                    weights.astype(jnp.bfloat16), values_all, preferred_element_type=jnp.float32
                )
                results.append(product / total)
            mixed = results[0]
            for side in range(1, 128 // HEAD_DIM):
                mixed = jnp.where((lane // HEAD_DIM) == side, results[side], mixed)
            mixed = mixed.astype(jnp.bfloat16)
            for place in range(bands):
                bstage[m, place, :, columns] = mixed[place * quad:(place + 1) * quad]
        for k in others:
            a2a_copy(m, k).start()
        blend[m, b] = bstage[m, b]

    def finish(m):
        for k in others:
            a2a_arrival(m, k).wait_recv()
        for start in range(0, width, 512):
            columns = slice(start, start + 512)
            total = full[m, b, :, columns].astype(jnp.float32)
            for group in range(bands):
                total += jnp.dot(
                    blend[m, group], wout[group, :, columns], preferred_element_type=jnp.float32
                )
            hstage[m, :, columns] = total.astype(jnp.bfloat16)

        @pl.when(s < last)
        def _():
            hidden_copy(m, 1).start()
            for k in others:
                ahead_copy(m, k).start()
            hidden_copy(m, 0).start()

        @pl.when(s == last)
        def _():
            fstage[m] = normalize(hstage[m], final_gain[...].reshape(1, width))
            for to in range(sections):
                final_copy(m, to, 1).start()
                if to != last:
                    final_copy(m, to, 0).start()
            final[m, :half] = fstage[m, half:]

    def decode(m):
        @pl.when(s < last)
        def _():
            final_arrival(m, 0).wait_recv()

        final_arrival(m, 1).wait_recv()
        decoded[m] = lax.dot_general(
            final[m], wdec[...], (((1,), (1,)), ((), ())), preferred_element_type=jnp.float32
        ).astype(jnp.bfloat16)

    row = labels[...].astype(jnp.float32)
    across = jnp.broadcast_to(row, bias.shape)

    load_out.wait()

    @pl.when(s == 0)
    def _():
        first_half.start()

    @pl.when(s == 1)
    def _():
        relay_first.start()

    bias[...] = jnp.where(across == across.T, 0.0, EXCLUDED)

    @pl.when(s == 1)
    def _():
        relay_first.serve(1)
        relay_second[0].start()
        relay_first.serve(2)
        relay_second[1].start()
        relay_first.serve(3)
        for distance in others:
            for chain in relay_second:
                chain.serve(distance)
            if distance == 2:
                for chain in weight_chains:
                    chain.start()

    @pl.when(s > 1)
    def _():
        for chain in weight_chains:
            chain.start()

    def serve_weights(distance):
        for chain in weight_chains:
            chain.serve(distance)

    @pl.when(s == 0)
    def _():
        first_half.serve(1)
        for chain in weight_chains:
            chain.start()
        first_half.serve(2)
        first_half.serve(3)

    @pl.when(s > 0)
    def _():
        for distance in others:
            serve_weights(distance)
        for m in range(micros):
            start_gather(m)

    def hand_over(m):
        @pl.when(s < last)
        def _():
            for k in others:
                ahead_arrival(m, k).wait_recv()
                ahead_forward(m, k).start()

    project(0)

    @pl.when(s == 0)
    def _():
        serve_weights(1)

    attend(0)

    @pl.when(s == 0)
    def _():
        serve_weights(2)
        serve_weights(3)

    weights_over_cores()
    weights_all()

    @pl.when(s < last)
    def _():
        finish(0)

    project(1)
    attend(1)

    @pl.when(s == last)
    def _():
        finish(0)

    hand_over(0)
    finish(1)
    hand_over(1)
    load_dec.wait()
    decode(0)
    decode(1)

    for m in range(micros):
        for k in others:
            a2a_copy(m, k).wait_send()
    for chain in weight_chains:
        chain.drain()
    for k in others:
        for chunk in chunks:
            wy_copy(k, chunk).wait_send()
            wc_copy(k, 0, chunk).wait_send()
            wc_copy(k, 1, chunk).wait_send()

    @pl.when(s == 0)
    def _():
        first_half.drain()

    @pl.when(s > 0)
    def _():
        for m in range(micros):
            for k in others:
                ag_copy(m, k, 1).wait_send()

    @pl.when(s == 1)
    def _():
        for chain in [relay_first, *relay_second]:
            chain.drain()
        for k in others:
            forward_copy(0, k, 1).wait_send()
            forward_copy(1, k, 0).wait_send()
            forward_copy(1, k, 1).wait_send()

    @pl.when(s < last)
    def _():
        for m in range(micros):
            for part in range(2):
                hidden_copy(m, part).wait_send()
            for k in others:
                ahead_copy(m, k).wait_send()
                ahead_forward(m, k).wait_send()

    @pl.when(s == last)
    def _():
        for m in range(micros):
            for to in range(sections):
                final_copy(m, to, 1).wait_send()
                if to != last:
                    final_copy(m, to, 0).wait_send()


def body(sections, windows, bands, tokens, regions, norm_gain, qkv_weight, out_weight, final_gain, dec_weight):
    micros, _, _, quad, width = tokens.shape
    inner = qkv_weight.shape[3]
    columns = dec_weight.shape[1]
    rows = bands * quad
    bf16 = jnp.bfloat16
    vmem = pl.BlockSpec(memory_space=pltpu.VMEM)
    hbm = pl.BlockSpec(memory_space=pl.ANY)
    dma = pltpu.SemaphoreType.DMA
    decoded = pl.pallas_call(
        functools.partial(kernel, sections, windows, bands),
        out_shape=jax.ShapeDtypeStruct((micros, quad, columns), bf16),
        in_specs=[vmem, vmem, vmem, hbm, hbm, vmem, hbm],
        out_specs=vmem,
        scratch_shapes=[
            pltpu.VMEM((micros, bands, quad, width), bf16),
            pltpu.VMEM((bands, quad // 2, width), bf16),
            pltpu.VMEM((bands, quad, width), bf16),
            pltpu.VMEM((micros, bands, quad // 2, width), bf16),
            pltpu.VMEM((rows, width), bf16),
            pltpu.VMEM((3, rows, inner), bf16),
            pltpu.VMEM((3, width, inner), bf16),
            pltpu.VMEM((bands, inner, width), bf16),
            pltpu.VMEM((columns, width), bf16),
            pltpu.VMEM((rows, rows), jnp.float32),
            pltpu.VMEM((micros, bands, quad, inner), bf16),
            pltpu.VMEM((micros, bands, quad, inner), bf16),
            pltpu.VMEM((micros, quad, width), bf16),
            pltpu.VMEM((micros, quad, width), bf16),
            pltpu.VMEM((micros, quad, width), bf16),
            dma((micros, 3)), dma((micros, 3, 2)),
            dma((micros, 3)), dma((micros, 3)),
            dma((micros, 2)), dma((micros, 2)),
            dma((micros, sections, 2)), dma((micros, 2)),
            dma((5, 2, 3)), dma((5, 2, 3)), dma((3, 3)),
            dma((micros, 3)), dma((micros, 3)), dma((micros, 3)),
            dma((2, 3)), dma((2, 3)),
            dma((2, 6)), dma((2, 6)),
            dma((3,)),
        ],
        compiler_params=pltpu.CompilerParams(
            collective_id=0, has_side_effects=True, vmem_limit_bytes=60 * 1024 * 1024
        ),
        name="relay",
    )(
        tokens[:, 0, 0],
        regions[0],
        norm_gain,
        jnp.transpose(qkv_weight[0], (1, 0, 2)),
        out_weight[0],
        final_gain,
        jnp.transpose(dec_weight),
    )
    return decoded[:, None, None]


def solution(mesh):
    sizes = mesh.shape
    return jax.shard_map(
        functools.partial(body, sizes["section"], sizes["win"], sizes["dp"]),
        mesh=mesh,
        in_specs=(
            P(None, "win", "dp", None, None),
            P("section", "win", None),
            P("section", None),
            P("section", None, None, "dp"),
            P("section", "dp", None),
            P(),
            P(None, "section"),
        ),
        out_specs=P(None, "win", "dp", None, "section"),
        check_vma=False,
    )
```

```python
import functools
import math

import jax
import jax.numpy as jnp
from jax import lax
from jax.experimental import pallas as pl
from jax.experimental.pallas import tpu as pltpu
from jax.sharding import PartitionSpec as P

HEAD_DIM = 64
MESH = pl.DeviceIdType.MESH
EXCLUDED = -1e30
QUARTERS_AHEAD = (2, 1)


def normalize(hidden, scales):
    values = hidden.astype(jnp.float32)
    center = values - jnp.mean(values, axis=-1, keepdims=True)
    spread = jnp.mean(center * center, axis=-1, keepdims=True)
    return (center * lax.rsqrt(spread + 1e-05) * scales).astype(jnp.bfloat16)


def kernel(
    sections, windows, bands,
    tokens, labels, gain, wqkv_hbm, wout_hbm, final_gain, wdec_hbm,
    decoded,
    full, relay_a, relay_b, ahead, normed, projected, wqkv, wout, wdec, bias, bstage, blend, hstage, fstage, final,
    ag_recv, a2a_send, a2a_recv, hid_send, hid_recv, fin_send, fin_recv,
    chain_send, chain_recv, fwd_send, nf_send, wy_send, wy_recv, wc_send, wc_recv, load_sem,
):
    micros, quad, width = tokens.shape
    half = quad // 2
    last = sections - 1
    s = lax.axis_index("section")
    w = lax.axis_index("win")
    b = lax.axis_index("dp")
    before = lax.rem(w + windows - 1, windows)
    after = lax.rem(w + 1, windows)
    core_peer = w + 1 - 2 * lax.rem(w, 2)
    chip_peer = w + 2 - 4 * lax.rem(w // 2, 2)
    quarter = lax.rem(w, 4)
    group_rows = wout_hbm.shape[0]
    piece = group_rows // 8

    def band(k):
        return lax.rem(b + k, bands)

    def send(src, dst, send_sem, recv_sem, device):
        return pltpu.make_async_remote_copy(
            src_ref=src, dst_ref=dst, send_sem=send_sem, recv_sem=recv_sem,
            device_id=device, device_id_type=MESH,
        )

    def part_of(m, slot, part):
        return full.at[m, slot, pl.ds(half * part, half)]

    def quarter_of(m, slot, q):
        return full.at[m, slot, pl.ds(half // 2 * q, half // 2)]

    def part_arrival(m, k, part):
        slot = part_of(m, band(k), part)
        return send(slot, slot, fwd_send.at[0, k - 1], ag_recv.at[m, k - 1, 2 * part], (s, w, band(k)))

    def quarter_arrival(m, k, q):
        slot = quarter_of(m, band(k), q)
        return send(slot, slot, fwd_send.at[0, k - 1], ag_recv.at[m, k - 1, q], (s, w, band(k)))

    class Chain:
        def __init__(self, index, slot, arrived):
            self.index, self.slot, self.arrived = index, slot, arrived

        def copy(self, way, distance, source):
            slot = self.slot(source)
            step = -1 if way else 1
            return send(slot, slot, chain_send.at[self.index, way, distance],
                        chain_recv.at[self.index, way, distance], (s, w, b + step))

        def each(self, distance, do):
            @pl.when((b >= distance) & (b < bands - 1))
            def _():
                do(self.copy(0, distance, b - distance))

            @pl.when((b + distance < bands) & (b > 0))
            def _():
                do(self.copy(1, distance, b + distance))

        def start(self):
            self.each(0, lambda copy: copy.start())

        def serve(self, distance):
            @pl.when(b >= distance)
            def _():
                self.copy(0, distance - 1, b - distance).wait_recv()

                if distance < bands - 1:
                    @pl.when(b < bands - 1)
                    def _():
                        self.copy(0, distance, b - distance).start()

                self.arrived(bands - distance)

            @pl.when(b + distance < bands)
            def _():
                self.copy(1, distance - 1, b + distance).wait_recv()

                if distance < bands - 1:
                    @pl.when(b > 0)
                    def _():
                        self.copy(1, distance, b + distance).start()

                self.arrived(distance)

        def drain(self):
            for distance in range(bands - 1):
                self.each(distance, lambda copy: copy.wait_send())

    def forward_copy(m, k, part):
        slot = relay_b.at[band(k), pl.ds(half * part, half)] if m else relay_a.at[band(k)]
        return send(slot, part_of(m, band(k), part), fwd_send.at[m + part if m else 0, k - 1],
                    ag_recv.at[m, k - 1, 2 * part], (0, w, b))

    def ahead_forward(m, k, q):
        rows = pl.ds(half // 2 * q, half // 2)
        return send(ahead.at[m, band(k), rows], quarter_of(m, band(k), q), nf_send.at[m, k - 1, q],
                    ag_recv.at[m, k - 1, q], (s + 1, w, b))

    def a2a_copy(m, k):
        return send(bstage.at[m, band(k)], blend.at[m, b], a2a_send.at[m, k - 1],
                    a2a_recv.at[m, bands - k - 1], (s, w, band(k)))

    def a2a_arrival(m, k):
        slot = blend.at[m, band(k)]
        return send(slot, slot, a2a_send.at[m, k - 1], a2a_recv.at[m, k - 1], (s, w, band(k)))

    def w_piece(slot, owner, chunk):
        start = (lax.rem(owner, 4) * 2 + chunk) * piece
        return wout.at[slot, pl.ds(pl.multiple_of(start, piece), piece)]

    def wy_copy(k, chunk):
        slot = w_piece(band(k), w, chunk)
        return send(slot, slot, wy_send.at[chunk, k - 1], wy_recv.at[chunk, k - 1], (s, chip_peer, b))

    def wy_arrival(k, chunk):
        slot = w_piece(band(k), chip_peer, chunk)
        return send(slot, slot, wy_send.at[chunk, k - 1], wy_recv.at[chunk, k - 1], (s, chip_peer, b))

    def wc_copy(k, far, chunk):
        slot = w_piece(band(k), chip_peer if far else w, chunk)
        index = 3 * far + k - 1
        return send(slot, slot, wc_send.at[chunk, index], wc_recv.at[chunk, index], (s, core_peer, b))

    def wc_arrival(k, far, chunk):
        other = core_peer + 2 - 4 * lax.rem(core_peer // 2, 2)
        slot = w_piece(band(k), other if far else core_peer, chunk)
        index = 3 * far + k - 1
        return send(slot, slot, wc_send.at[chunk, index], wc_recv.at[chunk, index], (s, core_peer, b))

    def hidden_copy(m, part):
        rows_from = pl.ds(half * (1 - part), half)
        rows_to = pl.ds(half * part, half)
        return send(hstage.at[m, rows_from], full.at[m, b, rows_to], hid_send.at[m, part],
                    hid_recv.at[m, part], (s + 1, before if part else w, b))

    def hidden_arrival(m, part):
        slot = full.at[m, b, pl.ds(half * part, half)]
        return send(slot, slot, hid_send.at[m, part], hid_recv.at[m, part], (s, after, b))

    def final_copy(m, to, part):
        rows_from = pl.ds(half * (1 - part), half)
        rows_to = pl.ds(half * part, half)
        return send(fstage.at[m, rows_from], final.at[m, rows_to], fin_send.at[m, to, part],
                    fin_recv.at[m, part], (to, before if part else w, b))

    def final_arrival(m, part):
        slot = final.at[m, pl.ds(half * part, half)]
        return send(slot, slot, fin_send.at[m, 0, part], fin_recv.at[m, part], (s, after, b))

    others = range(1, bands)
    chunks = range(2)

    gather_chains = [
        [
            Chain(5 + 4 * m + q, lambda slot, m=m, q=q: quarter_of(m, slot, q), lambda k: None)
            for q in (2, 3, 1, 0)[:4 - QUARTERS_AHEAD[m]]
        ]
        for m in range(micros)
    ]
    ahead_chains = [
        [
            Chain(13 + 2 * m + q,
                  lambda slot, m=m, q=q: ahead.at[m, slot, pl.ds(half // 2 * q, half // 2)],
                  lambda k, m=m, q=q: ahead_forward(m, k, q).start())
            for q in range(QUARTERS_AHEAD[m])
        ]
        for m in range(micros)
    ]

    def weights_arrived(chunk):
        def arrived(k):
            wy_copy(k, chunk).start()
            wc_copy(k, 0, chunk).start()
        return arrived

    def relayed(m, part):
        return lambda k: forward_copy(m, k, part).start()

    first_half = Chain(0, lambda slot: part_of(0, slot, 0), lambda k: None)
    relay_first = Chain(0, lambda slot: relay_a.at[slot], relayed(0, 1))
    weight_chains = [
        Chain(1 + c, lambda slot, c=c: w_piece(slot, w, c), weights_arrived(c)) for c in chunks
    ]
    relay_second = [
        Chain(3 + c, lambda slot, c=c: relay_b.at[slot, pl.ds(half * c, half)], relayed(1, c))
        for c in chunks
    ]

    load_qkv = pltpu.make_async_copy(wqkv_hbm, wqkv, load_sem.at[0])
    load_out = pltpu.make_async_copy(wout_hbm, wout.at[b], load_sem.at[1])
    load_dec = pltpu.make_async_copy(wdec_hbm, wdec, load_sem.at[2])
    load_qkv.start()
    load_out.start()
    load_dec.start()

    barrier = pltpu.get_barrier_semaphore()
    partners = [(s, w, band(k)) for k in others]
    partners += [(s, core_peer, b), (s, chip_peer, b)]
    partners += [(lax.rem(s + k, sections), w, b) for k in range(1, sections)]
    for to in range(sections):
        partners += [(to, before, b), (to, after, b)]
    for device in partners:
        pl.semaphore_signal(barrier, inc=1, device_id=device, device_id_type=MESH)

    @pl.when(s == 0)
    def _():
        for m in range(micros):
            full[m, b] = tokens[m]

    @pl.when(s == 1)
    def _():
        relay_a[b] = tokens[0, half:]
        relay_b[b] = tokens[1]

    pl.semaphore_wait(barrier, len(partners))

    def start_gather(m):
        hidden_arrival(m, 1).wait_recv()
        for chain in gather_chains[m][:2]:
            chain.start()
        hidden_arrival(m, 0).wait_recv()
        for chain in gather_chains[m][2:]:
            chain.start()

    def serve_gather(m, distance):
        for chain in gather_chains[m]:
            chain.serve(distance)

    def weights_over_cores():
        for k in others:
            for chunk in chunks:
                wy_arrival(k, chunk).wait_recv()
                wc_copy(k, 1, chunk).start()

    def weights_all():
        for k in others:
            for chunk in chunks:
                wc_arrival(k, 0, chunk).wait_recv()
                wc_arrival(k, 1, chunk).wait_recv()

    def normalize_band(m, slot):
        rows = pl.ds(pl.multiple_of(slot * quad, quad), quad)
        normed[rows, :] = normalize(full[m, slot], gain[...])

    def project(m):
        normalize_band(m, b)
        for k in others:
            @pl.when(s == 0)
            def _():
                for part in range(2):
                    if m + part > 0:
                        part_arrival(m, k, part).wait_recv()

            @pl.when(s > 0)
            def _():
                for q in range(QUARTERS_AHEAD[m]):
                    quarter_arrival(m, k, q).wait_recv()

            normalize_band(m, band(k))
        if m == 0:
            load_qkv.wait()
        for c in range(3):
            projected[c] = jnp.dot(
                normed[...], wqkv[c], preferred_element_type=jnp.float32
            ).astype(jnp.bfloat16)

    def attend(m):
        inner = projected.shape[2]
        rows = projected.shape[1]
        lane = lax.broadcasted_iota(jnp.int32, (rows, 128), 1)
        for pair in range(inner // 128):
            columns = slice(128 * pair, 128 * pair + 128)
            queries = projected[0, :, columns]
            keys_all = projected[1, :, columns]
            values_all = projected[2, :, columns]
            results = []
            for side in range(128 // HEAD_DIM):
                mine = (lane // HEAD_DIM) == side
                query = jnp.where(mine, queries, jnp.zeros_like(queries))
                scores = lax.dot_general(
                    query, keys_all, (((1,), (1,)), ((), ())), preferred_element_type=jnp.float32
                ) * (1.0 / math.sqrt(HEAD_DIM)) + bias[...]
                largest = jnp.max(scores, axis=-1, keepdims=True)
                weights = jnp.exp(scores - largest)
                total = jnp.sum(weights, axis=-1, keepdims=True)
                product = jnp.dot(
                    weights.astype(jnp.bfloat16), values_all, preferred_element_type=jnp.float32
                )
                results.append(product / total)
            mixed = results[0]
            for side in range(1, 128 // HEAD_DIM):
                mixed = jnp.where((lane // HEAD_DIM) == side, results[side], mixed)
            mixed = mixed.astype(jnp.bfloat16)
            for place in range(bands):
                bstage[m, place, :, columns] = mixed[place * quad:(place + 1) * quad]
        for k in others:
            a2a_copy(m, k).start()
        blend[m, b] = bstage[m, b]

    def finish(m):
        for k in others:
            a2a_arrival(m, k).wait_recv()
        for start in range(0, width, 512):
            columns = slice(start, start + 512)
            total = full[m, b, :, columns].astype(jnp.float32)
            for group in range(bands):
                total += jnp.dot(
                    blend[m, group], wout[group, :, columns], preferred_element_type=jnp.float32
                )
            hstage[m, :, columns] = total.astype(jnp.bfloat16)

        @pl.when(s < last)
        def _():
            hidden_copy(m, 1).start()
            ahead[m, b] = hstage[m, half:]
            for chain in ahead_chains[m]:
                chain.start()
            hidden_copy(m, 0).start()

        @pl.when(s == last)
        def _():
            fstage[m] = normalize(hstage[m], final_gain[...].reshape(1, width))
            for to in range(sections):
                final_copy(m, to, 1).start()
                if to != last:
                    final_copy(m, to, 0).start()
            final[m, :half] = fstage[m, half:]

    def decode(m):
        @pl.when(s < last)
        def _():
            final_arrival(m, 0).wait_recv()

        final_arrival(m, 1).wait_recv()
        decoded[m] = lax.dot_general(
            final[m], wdec[...], (((1,), (1,)), ((), ())), preferred_element_type=jnp.float32
        ).astype(jnp.bfloat16)

    row = labels[...].astype(jnp.float32)
    across = jnp.broadcast_to(row, bias.shape)

    load_out.wait()

    @pl.when(s == 0)
    def _():
        for chain in weight_chains:
            chain.start()

    @pl.when(s == 1)
    def _():
        relay_first.start()

    bias[...] = jnp.where(across == across.T, 0.0, EXCLUDED)

    @pl.when(s == 1)
    def _():
        relay_first.serve(1)
        relay_second[0].start()
        relay_first.serve(2)
        relay_second[1].start()
        relay_first.serve(3)
        for distance in others:
            for chain in relay_second:
                chain.serve(distance)
            if distance == 2:
                for chain in weight_chains:
                    chain.start()

    @pl.when(s > 1)
    def _():
        for chain in weight_chains:
            chain.start()

    for distance in others:
        for chain in weight_chains:
            chain.serve(distance)
        if distance == 2:
            @pl.when(s == 0)
            def _():
                first_half.start()

    @pl.when(s == 0)
    def _():
        for distance in others:
            first_half.serve(distance)
        weights_over_cores()

    @pl.when(s > 0)
    def _():
        start_gather(0)
        serve_gather(0, 1)
        serve_gather(0, 2)
        weights_over_cores()
        start_gather(1)
        serve_gather(0, 3)

    def hand_over(m):
        @pl.when(s < last)
        def _():
            for distance in others:
                for chain in ahead_chains[m]:
                    chain.serve(distance)

    project(0)

    @pl.when(s > 0)
    def _():
        serve_gather(1, 1)

    attend(0)

    @pl.when(s > 0)
    def _():
        serve_gather(1, 2)
        serve_gather(1, 3)

    weights_all()
    project(1)

    @pl.when(s < last)
    def _():
        finish(0)

    attend(1)

    @pl.when(s == last)
    def _():
        finish(0)

    hand_over(0)
    finish(1)
    hand_over(1)
    load_dec.wait()
    decode(0)
    decode(1)

    for m in range(micros):
        for k in others:
            a2a_copy(m, k).wait_send()
    for chain in weight_chains:
        chain.drain()
    for k in others:
        for chunk in chunks:
            wy_copy(k, chunk).wait_send()
            wc_copy(k, 0, chunk).wait_send()
            wc_copy(k, 1, chunk).wait_send()

    @pl.when(s == 0)
    def _():
        first_half.drain()

    @pl.when(s > 0)
    def _():
        for chain in gather_chains[0] + gather_chains[1]:
            chain.drain()

    @pl.when(s == 1)
    def _():
        for chain in [relay_first, *relay_second]:
            chain.drain()
        for k in others:
            forward_copy(0, k, 1).wait_send()
            forward_copy(1, k, 0).wait_send()
            forward_copy(1, k, 1).wait_send()

    @pl.when(s < last)
    def _():
        for m in range(micros):
            for part in range(2):
                hidden_copy(m, part).wait_send()
            for chain in ahead_chains[m]:
                chain.drain()
            for k in others:
                for q in range(QUARTERS_AHEAD[m]):
                    ahead_forward(m, k, q).wait_send()

    @pl.when(s == last)
    def _():
        for m in range(micros):
            for to in range(sections):
                final_copy(m, to, 1).wait_send()
                if to != last:
                    final_copy(m, to, 0).wait_send()


def body(sections, windows, bands, tokens, regions, norm_gain, qkv_weight, out_weight, final_gain, dec_weight):
    micros, _, _, quad, width = tokens.shape
    inner = qkv_weight.shape[3]
    columns = dec_weight.shape[1]
    rows = bands * quad
    bf16 = jnp.bfloat16
    vmem = pl.BlockSpec(memory_space=pltpu.VMEM)
    hbm = pl.BlockSpec(memory_space=pl.ANY)
    dma = pltpu.SemaphoreType.DMA
    decoded = pl.pallas_call(
        functools.partial(kernel, sections, windows, bands),
        out_shape=jax.ShapeDtypeStruct((micros, quad, columns), bf16),
        in_specs=[vmem, vmem, vmem, hbm, hbm, vmem, hbm],
        out_specs=vmem,
        scratch_shapes=[
            pltpu.VMEM((micros, bands, quad, width), bf16),
            pltpu.VMEM((bands, quad // 2, width), bf16),
            pltpu.VMEM((bands, quad, width), bf16),
            pltpu.VMEM((micros, bands, quad // 2, width), bf16),
            pltpu.VMEM((rows, width), bf16),
            pltpu.VMEM((3, rows, inner), bf16),
            pltpu.VMEM((3, width, inner), bf16),
            pltpu.VMEM((bands, inner, width), bf16),
            pltpu.VMEM((columns, width), bf16),
            pltpu.VMEM((rows, rows), jnp.float32),
            pltpu.VMEM((micros, bands, quad, inner), bf16),
            pltpu.VMEM((micros, bands, quad, inner), bf16),
            pltpu.VMEM((micros, quad, width), bf16),
            pltpu.VMEM((micros, quad, width), bf16),
            pltpu.VMEM((micros, quad, width), bf16),
            dma((micros, 3, 4)),
            dma((micros, 3)), dma((micros, 3)),
            dma((micros, 2)), dma((micros, 2)),
            dma((micros, sections, 2)), dma((micros, 2)),
            dma((17, 2, 3)), dma((17, 2, 3)), dma((3, 3)),
            dma((micros, 3, 2)),
            dma((2, 3)), dma((2, 3)),
            dma((2, 6)), dma((2, 6)),
            dma((3,)),
        ],
        compiler_params=pltpu.CompilerParams(
            collective_id=0, has_side_effects=True, vmem_limit_bytes=60 * 1024 * 1024
        ),
        name="relay",
    )(
        tokens[:, 0, 0],
        regions[0],
        norm_gain,
        jnp.transpose(qkv_weight[0], (1, 0, 2)),
        out_weight[0],
        final_gain,
        jnp.transpose(dec_weight),
    )
    return decoded[:, None, None]


def solution(mesh):
    sizes = mesh.shape
    return jax.shard_map(
        functools.partial(body, sizes["section"], sizes["win"], sizes["dp"]),
        mesh=mesh,
        in_specs=(
            P(None, "win", "dp", None, None),
            P("section", "win", None),
            P("section", None),
            P("section", None, None, "dp"),
            P("section", "dp", None),
            P(),
            P(None, "section"),
        ),
        out_specs=P(None, "win", "dp", None, "section"),
        check_vma=False,
    )
```

```python
import functools
import math

import jax
import jax.numpy as jnp
from jax import lax
from jax.experimental import pallas as pl
from jax.experimental.pallas import tpu as pltpu
from jax.sharding import PartitionSpec as P

HEAD_DIM = 64
MESH = pl.DeviceIdType.MESH
EXCLUDED = -1e30


def normalize(hidden, scales):
    values = hidden.astype(jnp.float32)
    center = values - jnp.mean(values, axis=-1, keepdims=True)
    spread = jnp.mean(center * center, axis=-1, keepdims=True)
    return (center * lax.rsqrt(spread + 1e-05) * scales).astype(jnp.bfloat16)


def kernel(
    sections, windows, bands,
    tokens, labels, gain, wqkv_hbm, wout_hbm, final_gain, wdec_hbm,
    decoded,
    full, relay_a, relay_b, ahead, normed, projected, wqkv, wout, wdec, bias, bstage, blend, hstage, fstage, final,
    ag_send, ag_recv, a2a_send, a2a_recv, hid_send, hid_recv, fin_send, fin_recv,
    chain_send, chain_recv, fwd_send, nx_send, nx_recv, nf_send, wy_send, wy_recv, wc_send, wc_recv, load_sem,
):
    micros, quad, width = tokens.shape
    half = quad // 2
    last = sections - 1
    s = lax.axis_index("section")
    w = lax.axis_index("win")
    b = lax.axis_index("dp")
    before = lax.rem(w + windows - 1, windows)
    after = lax.rem(w + 1, windows)
    core_peer = w + 1 - 2 * lax.rem(w, 2)
    chip_peer = w + 2 - 4 * lax.rem(w // 2, 2)
    quarter = lax.rem(w, 4)
    group_rows = wout_hbm.shape[0]
    piece = group_rows // 8

    def band(k):
        return lax.rem(b + k, bands)

    def send(src, dst, send_sem, recv_sem, device):
        return pltpu.make_async_remote_copy(
            src_ref=src, dst_ref=dst, send_sem=send_sem, recv_sem=recv_sem,
            device_id=device, device_id_type=MESH,
        )

    def part_of(m, slot, part):
        return full.at[m, slot, pl.ds(half * part, half)]

    def ag_copy(m, k, part):
        slot = part_of(m, b, part)
        return send(slot, slot, ag_send.at[m, k - 1],
                    ag_recv.at[m, bands - k - 1, part], (s, w, band(k)))

    def ag_arrival(m, k, part):
        slot = part_of(m, band(k), part)
        return send(slot, slot, ag_send.at[m, k - 1], ag_recv.at[m, k - 1, part], (s, w, band(k)))

    class Chain:
        def __init__(self, index, slot, arrived):
            self.index, self.slot, self.arrived = index, slot, arrived

        def copy(self, way, distance, source):
            slot = self.slot(source)
            step = -1 if way else 1
            return send(slot, slot, chain_send.at[self.index, way, distance],
                        chain_recv.at[self.index, way, distance], (s, w, b + step))

        def each(self, distance, do):
            @pl.when((b >= distance) & (b < bands - 1))
            def _():
                do(self.copy(0, distance, b - distance))

            @pl.when((b + distance < bands) & (b > 0))
            def _():
                do(self.copy(1, distance, b + distance))

        def start(self):
            self.each(0, lambda copy: copy.start())

        def serve(self, distance):
            @pl.when(b >= distance)
            def _():
                self.copy(0, distance - 1, b - distance).wait_recv()

                if distance < bands - 1:
                    @pl.when(b < bands - 1)
                    def _():
                        self.copy(0, distance, b - distance).start()

                self.arrived(bands - distance)

            @pl.when(b + distance < bands)
            def _():
                self.copy(1, distance - 1, b + distance).wait_recv()

                if distance < bands - 1:
                    @pl.when(b > 0)
                    def _():
                        self.copy(1, distance, b + distance).start()

                self.arrived(distance)

        def drain(self):
            for distance in range(bands - 1):
                self.each(distance, lambda copy: copy.wait_send())

    def forward_copy(m, k, part):
        slot = relay_b.at[band(k), pl.ds(half * part, half)] if m else relay_a.at[band(k)]
        return send(slot, part_of(m, band(k), part), fwd_send.at[m + part if m else 0, k - 1],
                    ag_recv.at[m, k - 1, part], (0, w, b))

    def ahead_copy(m, k):
        return send(hstage.at[m, pl.ds(half, half)], ahead.at[m, b], nx_send.at[m, k - 1],
                    nx_recv.at[m, bands - k - 1], (s, w, band(k)))

    def ahead_arrival(m, k):
        slot = ahead.at[m, band(k)]
        return send(slot, slot, nx_send.at[m, k - 1], nx_recv.at[m, k - 1], (s, w, band(k)))

    def ahead_forward(m, k):
        return send(ahead.at[m, band(k)], part_of(m, band(k), 0), nf_send.at[m, k - 1],
                    ag_recv.at[m, k - 1, 0], (s + 1, w, b))

    def a2a_copy(m, k):
        return send(bstage.at[m, band(k)], blend.at[m, b], a2a_send.at[m, k - 1],
                    a2a_recv.at[m, bands - k - 1], (s, w, band(k)))

    def a2a_arrival(m, k):
        slot = blend.at[m, band(k)]
        return send(slot, slot, a2a_send.at[m, k - 1], a2a_recv.at[m, k - 1], (s, w, band(k)))

    def w_piece(slot, owner, chunk):
        start = (lax.rem(owner, 4) * 2 + chunk) * piece
        return wout.at[slot, pl.ds(pl.multiple_of(start, piece), piece)]

    def wy_copy(k, chunk):
        slot = w_piece(band(k), w, chunk)
        return send(slot, slot, wy_send.at[chunk, k - 1], wy_recv.at[chunk, k - 1], (s, chip_peer, b))

    def wy_arrival(k, chunk):
        slot = w_piece(band(k), chip_peer, chunk)
        return send(slot, slot, wy_send.at[chunk, k - 1], wy_recv.at[chunk, k - 1], (s, chip_peer, b))

    def wc_copy(k, far, chunk):
        slot = w_piece(band(k), chip_peer if far else w, chunk)
        index = 3 * far + k - 1
        return send(slot, slot, wc_send.at[chunk, index], wc_recv.at[chunk, index], (s, core_peer, b))

    def wc_arrival(k, far, chunk):
        other = core_peer + 2 - 4 * lax.rem(core_peer // 2, 2)
        slot = w_piece(band(k), other if far else core_peer, chunk)
        index = 3 * far + k - 1
        return send(slot, slot, wc_send.at[chunk, index], wc_recv.at[chunk, index], (s, core_peer, b))

    def hidden_copy(m, part):
        rows_from = pl.ds(half * (1 - part), half)
        rows_to = pl.ds(half * part, half)
        return send(hstage.at[m, rows_from], full.at[m, b, rows_to], hid_send.at[m, part],
                    hid_recv.at[m, part], (s + 1, before if part else w, b))

    def hidden_arrival(m, part):
        slot = full.at[m, b, pl.ds(half * part, half)]
        return send(slot, slot, hid_send.at[m, part], hid_recv.at[m, part], (s, after, b))

    def final_copy(m, to, part):
        rows_from = pl.ds(half * (1 - part), half)
        rows_to = pl.ds(half * part, half)
        return send(fstage.at[m, rows_from], final.at[m, rows_to], fin_send.at[m, to, part],
                    fin_recv.at[m, part], (to, before if part else w, b))

    def final_arrival(m, part):
        slot = final.at[m, pl.ds(half * part, half)]
        return send(slot, slot, fin_send.at[m, 0, part], fin_recv.at[m, part], (s, after, b))

    others = range(1, bands)
    chunks = range(2)

    def weights_arrived(chunk):
        def arrived(k):
            wy_copy(k, chunk).start()
            wc_copy(k, 0, chunk).start()
        return arrived

    def relayed(m, part):
        return lambda k: forward_copy(m, k, part).start()

    first_half = Chain(0, lambda slot: part_of(0, slot, 0), lambda k: None)
    relay_first = Chain(0, lambda slot: relay_a.at[slot], relayed(0, 1))
    weight_chains = [
        Chain(1 + c, lambda slot, c=c: w_piece(slot, w, c), weights_arrived(c)) for c in chunks
    ]
    relay_second = [
        Chain(3 + c, lambda slot, c=c: relay_b.at[slot, pl.ds(half * c, half)], relayed(1, c))
        for c in chunks
    ]

    load_qkv = pltpu.make_async_copy(wqkv_hbm, wqkv, load_sem.at[0])
    load_out = pltpu.make_async_copy(wout_hbm, wout.at[b], load_sem.at[1])
    load_dec = pltpu.make_async_copy(wdec_hbm, wdec, load_sem.at[2])
    load_qkv.start()
    load_out.start()
    load_dec.start()

    barrier = pltpu.get_barrier_semaphore()
    partners = [(s, w, band(k)) for k in others]
    partners += [(s, core_peer, b), (s, chip_peer, b)]
    partners += [(lax.rem(s + k, sections), w, b) for k in range(1, sections)]
    for to in range(sections):
        partners += [(to, before, b), (to, after, b)]
    for device in partners:
        pl.semaphore_signal(barrier, inc=1, device_id=device, device_id_type=MESH)

    @pl.when(s == 0)
    def _():
        for m in range(micros):
            full[m, b] = tokens[m]

    @pl.when(s == 1)
    def _():
        relay_a[b] = tokens[0, half:]
        relay_b[b] = tokens[1]

    pl.semaphore_wait(barrier, len(partners))

    def start_gather(m):
        hidden_arrival(m, 1).wait_recv()
        for k in others:
            ag_copy(m, k, 1).start()
        hidden_arrival(m, 0).wait_recv()

    def weights_over_cores():
        for k in others:
            for chunk in chunks:
                wy_arrival(k, chunk).wait_recv()
                wc_copy(k, 1, chunk).start()

    def weights_all():
        for k in others:
            for chunk in chunks:
                wc_arrival(k, 0, chunk).wait_recv()
                wc_arrival(k, 1, chunk).wait_recv()

    def normalize_band(m, slot):
        rows = pl.ds(pl.multiple_of(slot * quad, quad), quad)
        normed[rows, :] = normalize(full[m, slot], gain[...])

    def project(m):
        normalize_band(m, b)
        for k in others:
            if m == 0:
                @pl.when(s > 0)
                def _():
                    ag_arrival(m, k, 0).wait_recv()
            else:
                ag_arrival(m, k, 0).wait_recv()
            ag_arrival(m, k, 1).wait_recv()
            normalize_band(m, band(k))
        if m == 0:
            load_qkv.wait()
        for c in range(3):
            projected[c] = jnp.dot(
                normed[...], wqkv[c], preferred_element_type=jnp.float32
            ).astype(jnp.bfloat16)

    def attend(m):
        inner = projected.shape[2]
        rows = projected.shape[1]
        lane = lax.broadcasted_iota(jnp.int32, (rows, 128), 1)
        for pair in range(inner // 128):
            columns = slice(128 * pair, 128 * pair + 128)
            queries = projected[0, :, columns]
            keys_all = projected[1, :, columns]
            values_all = projected[2, :, columns]
            results = []
            for side in range(128 // HEAD_DIM):
                mine = (lane // HEAD_DIM) == side
                query = jnp.where(mine, queries, jnp.zeros_like(queries))
                scores = lax.dot_general(
                    query, keys_all, (((1,), (1,)), ((), ())), preferred_element_type=jnp.float32
                ) * (1.0 / math.sqrt(HEAD_DIM)) + bias[...]
                largest = jnp.max(scores, axis=-1, keepdims=True)
                weights = jnp.exp(scores - largest)
                total = jnp.sum(weights, axis=-1, keepdims=True)
                product = jnp.dot(
                    weights.astype(jnp.bfloat16), values_all, preferred_element_type=jnp.float32
                )
                results.append(product / total)
            mixed = results[0]
            for side in range(1, 128 // HEAD_DIM):
                mixed = jnp.where((lane // HEAD_DIM) == side, results[side], mixed)
            mixed = mixed.astype(jnp.bfloat16)
            for place in range(bands):
                bstage[m, place, :, columns] = mixed[place * quad:(place + 1) * quad]
        for k in others:
            a2a_copy(m, k).start()
        blend[m, b] = bstage[m, b]

    def finish(m):
        for k in others:
            a2a_arrival(m, k).wait_recv()
        for start in range(0, width, 512):
            columns = slice(start, start + 512)
            total = full[m, b, :, columns].astype(jnp.float32)
            for group in range(bands):
                total += jnp.dot(
                    blend[m, group], wout[group, :, columns], preferred_element_type=jnp.float32
                )
            hstage[m, :, columns] = total.astype(jnp.bfloat16)

        @pl.when(s < last)
        def _():
            hidden_copy(m, 1).start()
            for k in others:
                ahead_copy(m, k).start()
            hidden_copy(m, 0).start()

        @pl.when(s == last)
        def _():
            fstage[m] = normalize(hstage[m], final_gain[...].reshape(1, width))
            for to in range(sections):
                final_copy(m, to, 1).start()
                if to != last:
                    final_copy(m, to, 0).start()
            final[m, :half] = fstage[m, half:]

    def decode(m):
        @pl.when(s < last)
        def _():
            final_arrival(m, 0).wait_recv()

        final_arrival(m, 1).wait_recv()
        decoded[m] = lax.dot_general(
            final[m], wdec[...], (((1,), (1,)), ((), ())), preferred_element_type=jnp.float32
        ).astype(jnp.bfloat16)

    row = labels[...].astype(jnp.float32)
    across = jnp.broadcast_to(row, bias.shape)

    load_out.wait()

    @pl.when(s == 0)
    def _():
        for chain in weight_chains:
            chain.start()

    @pl.when(s == 1)
    def _():
        relay_first.start()

    bias[...] = jnp.where(across == across.T, 0.0, EXCLUDED)

    @pl.when(s == 1)
    def _():
        relay_first.serve(1)
        relay_second[0].start()
        relay_first.serve(2)
        relay_second[1].start()
        relay_first.serve(3)
        for distance in others:
            for chain in relay_second:
                chain.serve(distance)
            if distance == 2:
                for chain in weight_chains:
                    chain.start()

    @pl.when(s > 1)
    def _():
        for chain in weight_chains:
            chain.start()

    for distance in others:
        for chain in weight_chains:
            chain.serve(distance)
        if distance == 2:
            @pl.when(s == 0)
            def _():
                first_half.start()

    @pl.when(s == 0)
    def _():
        for distance in others:
            first_half.serve(distance)
        weights_over_cores()

    @pl.when(s > 0)
    def _():
        for m in range(micros):
            start_gather(m)
        weights_over_cores()

    def hand_over(m):
        @pl.when(s < last)
        def _():
            for k in others:
                ahead_arrival(m, k).wait_recv()
                ahead_forward(m, k).start()

    project(0)
    attend(0)
    weights_all()
    project(1)

    @pl.when(s < last)
    def _():
        finish(0)

    attend(1)

    @pl.when(s == last)
    def _():
        finish(0)

    finish(1)
    hand_over(0)
    hand_over(1)
    load_dec.wait()
    decode(0)
    decode(1)

    for m in range(micros):
        for k in others:
            a2a_copy(m, k).wait_send()
    for chain in weight_chains:
        chain.drain()
    for k in others:
        for chunk in chunks:
            wy_copy(k, chunk).wait_send()
            wc_copy(k, 0, chunk).wait_send()
            wc_copy(k, 1, chunk).wait_send()

    @pl.when(s == 0)
    def _():
        first_half.drain()

    @pl.when(s > 0)
    def _():
        for m in range(micros):
            for k in others:
                ag_copy(m, k, 1).wait_send()

    @pl.when(s == 1)
    def _():
        for chain in [relay_first, *relay_second]:
            chain.drain()
        for k in others:
            forward_copy(0, k, 1).wait_send()
            forward_copy(1, k, 0).wait_send()
            forward_copy(1, k, 1).wait_send()

    @pl.when(s < last)
    def _():
        for m in range(micros):
            for part in range(2):
                hidden_copy(m, part).wait_send()
            for k in others:
                ahead_copy(m, k).wait_send()
                ahead_forward(m, k).wait_send()

    @pl.when(s == last)
    def _():
        for m in range(micros):
            for to in range(sections):
                final_copy(m, to, 1).wait_send()
                if to != last:
                    final_copy(m, to, 0).wait_send()


def body(sections, windows, bands, tokens, regions, norm_gain, qkv_weight, out_weight, final_gain, dec_weight):
    micros, _, _, quad, width = tokens.shape
    inner = qkv_weight.shape[3]
    columns = dec_weight.shape[1]
    rows = bands * quad
    bf16 = jnp.bfloat16
    vmem = pl.BlockSpec(memory_space=pltpu.VMEM)
    hbm = pl.BlockSpec(memory_space=pl.ANY)
    dma = pltpu.SemaphoreType.DMA
    decoded = pl.pallas_call(
        functools.partial(kernel, sections, windows, bands),
        out_shape=jax.ShapeDtypeStruct((micros, quad, columns), bf16),
        in_specs=[vmem, vmem, vmem, hbm, hbm, vmem, hbm],
        out_specs=vmem,
        scratch_shapes=[
            pltpu.VMEM((micros, bands, quad, width), bf16),
            pltpu.VMEM((bands, quad // 2, width), bf16),
            pltpu.VMEM((bands, quad, width), bf16),
            pltpu.VMEM((micros, bands, quad // 2, width), bf16),
            pltpu.VMEM((rows, width), bf16),
            pltpu.VMEM((3, rows, inner), bf16),
            pltpu.VMEM((3, width, inner), bf16),
            pltpu.VMEM((bands, inner, width), bf16),
            pltpu.VMEM((columns, width), bf16),
            pltpu.VMEM((rows, rows), jnp.float32),
            pltpu.VMEM((micros, bands, quad, inner), bf16),
            pltpu.VMEM((micros, bands, quad, inner), bf16),
            pltpu.VMEM((micros, quad, width), bf16),
            pltpu.VMEM((micros, quad, width), bf16),
            pltpu.VMEM((micros, quad, width), bf16),
            dma((micros, 3)), dma((micros, 3, 2)),
            dma((micros, 3)), dma((micros, 3)),
            dma((micros, 2)), dma((micros, 2)),
            dma((micros, sections, 2)), dma((micros, 2)),
            dma((5, 2, 3)), dma((5, 2, 3)), dma((3, 3)),
            dma((micros, 3)), dma((micros, 3)), dma((micros, 3)),
            dma((2, 3)), dma((2, 3)),
            dma((2, 6)), dma((2, 6)),
            dma((3,)),
        ],
        compiler_params=pltpu.CompilerParams(
            collective_id=0, has_side_effects=True, vmem_limit_bytes=60 * 1024 * 1024
        ),
        name="relay",
    )(
        tokens[:, 0, 0],
        regions[0],
        norm_gain,
        jnp.transpose(qkv_weight[0], (1, 0, 2)),
        out_weight[0],
        final_gain,
        jnp.transpose(dec_weight),
    )
    return decoded[:, None, None]


def solution(mesh):
    sizes = mesh.shape
    return jax.shard_map(
        functools.partial(body, sizes["section"], sizes["win"], sizes["dp"]),
        mesh=mesh,
        in_specs=(
            P(None, "win", "dp", None, None),
            P("section", "win", None),
            P("section", None),
            P("section", None, None, "dp"),
            P("section", "dp", None),
            P(),
            P(None, "section"),
        ),
        out_specs=P(None, "win", "dp", None, "section"),
        check_vma=False,
    )
```

```python
import functools
import math

import jax
import jax.numpy as jnp
from jax import lax
from jax.experimental import pallas as pl
from jax.experimental.pallas import tpu as pltpu
from jax.sharding import PartitionSpec as P

HEAD_DIM = 64
MESH = pl.DeviceIdType.MESH
EXCLUDED = -1e30


def normalize(hidden, scales):
    values = hidden.astype(jnp.float32)
    center = values - jnp.mean(values, axis=-1, keepdims=True)
    spread = jnp.mean(center * center, axis=-1, keepdims=True)
    return (center * lax.rsqrt(spread + 1e-05) * scales).astype(jnp.bfloat16)


def kernel(
    sections, windows, bands,
    tokens, labels, gain, wqkv_hbm, wout_hbm, final_gain, wdec_hbm,
    decoded,
    full, relay_a, relay_b, ahead, normed, projected, wqkv, wout, wdec, bias, bstage, blend, hstage, fstage, final,
    ag_send, ag_recv, a2a_send, a2a_recv, hid_send, hid_recv, fin_send, fin_recv,
    chain_send, chain_recv, fwd_send, nx_send, nx_recv, nf_send, wy_send, wy_recv, wc_send, wc_recv, load_sem,
):
    micros, quad, width = tokens.shape
    half = quad // 2
    last = sections - 1
    s = lax.axis_index("section")
    w = lax.axis_index("win")
    b = lax.axis_index("dp")
    before = lax.rem(w + windows - 1, windows)
    after = lax.rem(w + 1, windows)
    core_peer = w + 1 - 2 * lax.rem(w, 2)
    chip_peer = w + 2 - 4 * lax.rem(w // 2, 2)
    quarter = lax.rem(w, 4)
    group_rows = wout_hbm.shape[0]
    piece = group_rows // 8

    def band(k):
        return lax.rem(b + k, bands)

    def send(src, dst, send_sem, recv_sem, device):
        return pltpu.make_async_remote_copy(
            src_ref=src, dst_ref=dst, send_sem=send_sem, recv_sem=recv_sem,
            device_id=device, device_id_type=MESH,
        )

    def part_of(m, slot, part):
        return full.at[m, slot, pl.ds(half * part, half)]

    def ag_copy(m, k, part):
        slot = part_of(m, b, part)
        return send(slot, slot, ag_send.at[m, k - 1],
                    ag_recv.at[m, bands - k - 1, part], (s, w, band(k)))

    def ag_arrival(m, k, part):
        slot = part_of(m, band(k), part)
        return send(slot, slot, ag_send.at[m, k - 1], ag_recv.at[m, k - 1, part], (s, w, band(k)))

    class Chain:
        def __init__(self, index, slot, arrived):
            self.index, self.slot, self.arrived = index, slot, arrived

        def copy(self, way, distance, source):
            slot = self.slot(source)
            step = -1 if way else 1
            return send(slot, slot, chain_send.at[self.index, way, distance],
                        chain_recv.at[self.index, way, distance], (s, w, b + step))

        def each(self, distance, do):
            @pl.when((b >= distance) & (b < bands - 1))
            def _():
                do(self.copy(0, distance, b - distance))

            @pl.when((b + distance < bands) & (b > 0))
            def _():
                do(self.copy(1, distance, b + distance))

        def start(self):
            self.each(0, lambda copy: copy.start())

        def serve(self, distance):
            @pl.when(b >= distance)
            def _():
                self.copy(0, distance - 1, b - distance).wait_recv()

                if distance < bands - 1:
                    @pl.when(b < bands - 1)
                    def _():
                        self.copy(0, distance, b - distance).start()

                self.arrived(bands - distance)

            @pl.when(b + distance < bands)
            def _():
                self.copy(1, distance - 1, b + distance).wait_recv()

                if distance < bands - 1:
                    @pl.when(b > 0)
                    def _():
                        self.copy(1, distance, b + distance).start()

                self.arrived(distance)

        def drain(self):
            for distance in range(bands - 1):
                self.each(distance, lambda copy: copy.wait_send())

    def forward_copy(m, k, part):
        slot = relay_b.at[band(k), pl.ds(half * part, half)] if m else relay_a.at[band(k)]
        return send(slot, part_of(m, band(k), part), fwd_send.at[m + part if m else 0, k - 1],
                    ag_recv.at[m, k - 1, part], (0, w, b))

    def ahead_copy(m, k):
        return send(hstage.at[m, pl.ds(half, half)], ahead.at[m, b], nx_send.at[m, k - 1],
                    nx_recv.at[m, bands - k - 1], (s, w, band(k)))

    def ahead_arrival(m, k):
        slot = ahead.at[m, band(k)]
        return send(slot, slot, nx_send.at[m, k - 1], nx_recv.at[m, k - 1], (s, w, band(k)))

    def ahead_forward(m, k):
        return send(ahead.at[m, band(k)], part_of(m, band(k), 0), nf_send.at[m, k - 1],
                    ag_recv.at[m, k - 1, 0], (s + 1, w, b))

    def a2a_copy(m, k):
        return send(bstage.at[m, band(k)], blend.at[m, b], a2a_send.at[m, k - 1],
                    a2a_recv.at[m, bands - k - 1], (s, w, band(k)))

    def a2a_arrival(m, k):
        slot = blend.at[m, band(k)]
        return send(slot, slot, a2a_send.at[m, k - 1], a2a_recv.at[m, k - 1], (s, w, band(k)))

    def w_piece(slot, owner, chunk):
        start = (lax.rem(owner, 4) * 2 + chunk) * piece
        return wout.at[slot, pl.ds(pl.multiple_of(start, piece), piece)]

    def wy_copy(k, chunk):
        slot = w_piece(band(k), w, chunk)
        return send(slot, slot, wy_send.at[chunk, k - 1], wy_recv.at[chunk, k - 1], (s, chip_peer, b))

    def wy_arrival(k, chunk):
        slot = w_piece(band(k), chip_peer, chunk)
        return send(slot, slot, wy_send.at[chunk, k - 1], wy_recv.at[chunk, k - 1], (s, chip_peer, b))

    def wc_copy(k, far, chunk):
        slot = w_piece(band(k), chip_peer if far else w, chunk)
        index = 3 * far + k - 1
        return send(slot, slot, wc_send.at[chunk, index], wc_recv.at[chunk, index], (s, core_peer, b))

    def wc_arrival(k, far, chunk):
        other = core_peer + 2 - 4 * lax.rem(core_peer // 2, 2)
        slot = w_piece(band(k), other if far else core_peer, chunk)
        index = 3 * far + k - 1
        return send(slot, slot, wc_send.at[chunk, index], wc_recv.at[chunk, index], (s, core_peer, b))

    def hidden_copy(m, part):
        rows_from = pl.ds(half * (1 - part), half)
        rows_to = pl.ds(half * part, half)
        return send(hstage.at[m, rows_from], full.at[m, b, rows_to], hid_send.at[m, part],
                    hid_recv.at[m, part], (s + 1, before if part else w, b))

    def hidden_arrival(m, part):
        slot = full.at[m, b, pl.ds(half * part, half)]
        return send(slot, slot, hid_send.at[m, part], hid_recv.at[m, part], (s, after, b))

    def final_copy(m, to, part):
        rows_from = pl.ds(half * (1 - part), half)
        rows_to = pl.ds(half * part, half)
        return send(fstage.at[m, rows_from], final.at[m, rows_to], fin_send.at[m, to, part],
                    fin_recv.at[m, part], (to, before if part else w, b))

    def final_arrival(m, part):
        slot = final.at[m, pl.ds(half * part, half)]
        return send(slot, slot, fin_send.at[m, 0, part], fin_recv.at[m, part], (s, after, b))

    others = range(1, bands)
    chunks = range(2)

    def weights_arrived(chunk):
        def arrived(k):
            wy_copy(k, chunk).start()
            wc_copy(k, 0, chunk).start()
        return arrived

    def relayed(m, part):
        return lambda k: forward_copy(m, k, part).start()

    first_half = Chain(0, lambda slot: part_of(0, slot, 0), lambda k: None)
    relay_first = Chain(0, lambda slot: relay_a.at[slot], relayed(0, 1))
    weight_chains = [
        Chain(1 + c, lambda slot, c=c: w_piece(slot, w, c), weights_arrived(c)) for c in chunks
    ]
    relay_second = [
        Chain(3 + c, lambda slot, c=c: relay_b.at[slot, pl.ds(half * c, half)], relayed(1, c))
        for c in chunks
    ]

    load_qkv = pltpu.make_async_copy(wqkv_hbm, wqkv, load_sem.at[0])
    load_out = pltpu.make_async_copy(wout_hbm, wout.at[b], load_sem.at[1])
    load_dec = pltpu.make_async_copy(wdec_hbm, wdec, load_sem.at[2])
    load_qkv.start()
    load_out.start()
    load_dec.start()

    barrier = pltpu.get_barrier_semaphore()
    partners = [(s, w, band(k)) for k in others]
    partners += [(s, core_peer, b), (s, chip_peer, b)]
    partners += [(lax.rem(s + k, sections), w, b) for k in range(1, sections)]
    for to in range(sections):
        partners += [(to, before, b), (to, after, b)]
    for device in partners:
        pl.semaphore_signal(barrier, inc=1, device_id=device, device_id_type=MESH)

    @pl.when(s == 0)
    def _():
        for m in range(micros):
            full[m, b] = tokens[m]

    @pl.when(s == 1)
    def _():
        relay_a[b] = tokens[0, half:]
        relay_b[b] = tokens[1]

    pl.semaphore_wait(barrier, len(partners))

    def start_gather(m):
        hidden_arrival(m, 1).wait_recv()
        for k in others:
            ag_copy(m, k, 1).start()
        hidden_arrival(m, 0).wait_recv()

    def weights_over_cores():
        for k in others:
            for chunk in chunks:
                wy_arrival(k, chunk).wait_recv()
                wc_copy(k, 1, chunk).start()

    def weights_all():
        for k in others:
            for chunk in chunks:
                wc_arrival(k, 0, chunk).wait_recv()
                wc_arrival(k, 1, chunk).wait_recv()

    def normalize_band(m, slot):
        rows = pl.ds(pl.multiple_of(slot * quad, quad), quad)
        normed[rows, :] = normalize(full[m, slot], gain[...])

    def project(m):
        normalize_band(m, b)
        for k in others:
            if m == 0:
                @pl.when(s > 0)
                def _():
                    ag_arrival(m, k, 0).wait_recv()
            else:
                ag_arrival(m, k, 0).wait_recv()
            ag_arrival(m, k, 1).wait_recv()
            normalize_band(m, band(k))
        if m == 0:
            load_qkv.wait()
        for c in range(3):
            projected[c] = jnp.dot(
                normed[...], wqkv[c], preferred_element_type=jnp.float32
            ).astype(jnp.bfloat16)

    def attend(m):
        inner = projected.shape[2]
        rows = projected.shape[1]
        lane = lax.broadcasted_iota(jnp.int32, (rows, 128), 1)
        for pair in range(inner // 128):
            columns = slice(128 * pair, 128 * pair + 128)
            queries = projected[0, :, columns]
            keys_all = projected[1, :, columns]
            values_all = projected[2, :, columns]
            results = []
            for side in range(128 // HEAD_DIM):
                mine = (lane // HEAD_DIM) == side
                query = jnp.where(mine, queries, jnp.zeros_like(queries))
                scores = lax.dot_general(
                    query, keys_all, (((1,), (1,)), ((), ())), preferred_element_type=jnp.float32
                ) * (1.0 / math.sqrt(HEAD_DIM)) + bias[...]
                largest = jnp.max(scores, axis=-1, keepdims=True)
                weights = jnp.exp(scores - largest)
                total = jnp.sum(weights, axis=-1, keepdims=True)
                product = jnp.dot(
                    weights.astype(jnp.bfloat16), values_all, preferred_element_type=jnp.float32
                )
                results.append(product / total)
            mixed = results[0]
            for side in range(1, 128 // HEAD_DIM):
                mixed = jnp.where((lane // HEAD_DIM) == side, results[side], mixed)
            mixed = mixed.astype(jnp.bfloat16)
            for place in range(bands):
                bstage[m, place, :, columns] = mixed[place * quad:(place + 1) * quad]
        for k in others:
            a2a_copy(m, k).start()
        blend[m, b] = bstage[m, b]

    def finish(m):
        for k in others:
            a2a_arrival(m, k).wait_recv()
        for start in range(0, width, 512):
            columns = slice(start, start + 512)
            total = full[m, b, :, columns].astype(jnp.float32)
            for group in range(bands):
                total += jnp.dot(
                    blend[m, group], wout[group, :, columns], preferred_element_type=jnp.float32
                )
            hstage[m, :, columns] = total.astype(jnp.bfloat16)

        @pl.when(s < last)
        def _():
            hidden_copy(m, 1).start()
            for k in others:
                ahead_copy(m, k).start()
            hidden_copy(m, 0).start()

        @pl.when(s == last)
        def _():
            fstage[m] = normalize(hstage[m], final_gain[...].reshape(1, width))
            for to in range(sections):
                final_copy(m, to, 1).start()
                if to != last:
                    final_copy(m, to, 0).start()
            final[m, :half] = fstage[m, half:]

    def decode(m):
        @pl.when(s < last)
        def _():
            final_arrival(m, 0).wait_recv()

        final_arrival(m, 1).wait_recv()
        decoded[m] = lax.dot_general(
            final[m], wdec[...], (((1,), (1,)), ((), ())), preferred_element_type=jnp.float32
        ).astype(jnp.bfloat16)

    row = labels[...].astype(jnp.float32)
    across = jnp.broadcast_to(row, bias.shape)

    load_out.wait()

    @pl.when(s == 0)
    def _():
        for chain in [first_half, *weight_chains]:
            chain.start()

    @pl.when(s == 1)
    def _():
        relay_first.start()

    bias[...] = jnp.where(across == across.T, 0.0, EXCLUDED)

    @pl.when(s == 1)
    def _():
        relay_first.serve(1)
        relay_second[0].start()
        relay_first.serve(2)
        relay_second[1].start()
        relay_first.serve(3)
        for distance in others:
            for chain in relay_second:
                chain.serve(distance)
            if distance == 2:
                for chain in weight_chains:
                    chain.start()

    @pl.when(s > 1)
    def _():
        for chain in weight_chains:
            chain.start()

    for distance in others:
        for chain in weight_chains:
            chain.serve(distance)

        @pl.when(s == 0)
        def _():
            first_half.serve(distance)

    @pl.when(s == 0)
    def _():
        weights_over_cores()

    @pl.when(s > 0)
    def _():
        for m in range(micros):
            start_gather(m)
        weights_over_cores()

    def hand_over(m):
        @pl.when(s < last)
        def _():
            for k in others:
                ahead_arrival(m, k).wait_recv()
                ahead_forward(m, k).start()

    project(0)
    attend(0)
    weights_all()
    project(1)

    @pl.when(s < last)
    def _():
        finish(0)

    attend(1)

    @pl.when(s == last)
    def _():
        finish(0)

    hand_over(0)
    finish(1)
    hand_over(1)
    load_dec.wait()
    decode(0)
    decode(1)

    for m in range(micros):
        for k in others:
            a2a_copy(m, k).wait_send()
    for chain in weight_chains:
        chain.drain()
    for k in others:
        for chunk in chunks:
            wy_copy(k, chunk).wait_send()
            wc_copy(k, 0, chunk).wait_send()
            wc_copy(k, 1, chunk).wait_send()

    @pl.when(s == 0)
    def _():
        first_half.drain()

    @pl.when(s > 0)
    def _():
        for m in range(micros):
            for k in others:
                ag_copy(m, k, 1).wait_send()

    @pl.when(s == 1)
    def _():
        for chain in [relay_first, *relay_second]:
            chain.drain()
        for k in others:
            forward_copy(0, k, 1).wait_send()
            forward_copy(1, k, 0).wait_send()
            forward_copy(1, k, 1).wait_send()

    @pl.when(s < last)
    def _():
        for m in range(micros):
            for part in range(2):
                hidden_copy(m, part).wait_send()
            for k in others:
                ahead_copy(m, k).wait_send()
                ahead_forward(m, k).wait_send()

    @pl.when(s == last)
    def _():
        for m in range(micros):
            for to in range(sections):
                final_copy(m, to, 1).wait_send()
                if to != last:
                    final_copy(m, to, 0).wait_send()


def body(sections, windows, bands, tokens, regions, norm_gain, qkv_weight, out_weight, final_gain, dec_weight):
    micros, _, _, quad, width = tokens.shape
    inner = qkv_weight.shape[3]
    columns = dec_weight.shape[1]
    rows = bands * quad
    bf16 = jnp.bfloat16
    vmem = pl.BlockSpec(memory_space=pltpu.VMEM)
    hbm = pl.BlockSpec(memory_space=pl.ANY)
    dma = pltpu.SemaphoreType.DMA
    decoded = pl.pallas_call(
        functools.partial(kernel, sections, windows, bands),
        out_shape=jax.ShapeDtypeStruct((micros, quad, columns), bf16),
        in_specs=[vmem, vmem, vmem, hbm, hbm, vmem, hbm],
        out_specs=vmem,
        scratch_shapes=[
            pltpu.VMEM((micros, bands, quad, width), bf16),
            pltpu.VMEM((bands, quad // 2, width), bf16),
            pltpu.VMEM((bands, quad, width), bf16),
            pltpu.VMEM((micros, bands, quad // 2, width), bf16),
            pltpu.VMEM((rows, width), bf16),
            pltpu.VMEM((3, rows, inner), bf16),
            pltpu.VMEM((3, width, inner), bf16),
            pltpu.VMEM((bands, inner, width), bf16),
            pltpu.VMEM((columns, width), bf16),
            pltpu.VMEM((rows, rows), jnp.float32),
            pltpu.VMEM((micros, bands, quad, inner), bf16),
            pltpu.VMEM((micros, bands, quad, inner), bf16),
            pltpu.VMEM((micros, quad, width), bf16),
            pltpu.VMEM((micros, quad, width), bf16),
            pltpu.VMEM((micros, quad, width), bf16),
            dma((micros, 3)), dma((micros, 3, 2)),
            dma((micros, 3)), dma((micros, 3)),
            dma((micros, 2)), dma((micros, 2)),
            dma((micros, sections, 2)), dma((micros, 2)),
            dma((5, 2, 3)), dma((5, 2, 3)), dma((3, 3)),
            dma((micros, 3)), dma((micros, 3)), dma((micros, 3)),
            dma((2, 3)), dma((2, 3)),
            dma((2, 6)), dma((2, 6)),
            dma((3,)),
        ],
        compiler_params=pltpu.CompilerParams(
            collective_id=0, has_side_effects=True, vmem_limit_bytes=60 * 1024 * 1024
        ),
        name="relay",
    )(
        tokens[:, 0, 0],
        regions[0],
        norm_gain,
        jnp.transpose(qkv_weight[0], (1, 0, 2)),
        out_weight[0],
        final_gain,
        jnp.transpose(dec_weight),
    )
    return decoded[:, None, None]


def solution(mesh):
    sizes = mesh.shape
    return jax.shard_map(
        functools.partial(body, sizes["section"], sizes["win"], sizes["dp"]),
        mesh=mesh,
        in_specs=(
            P(None, "win", "dp", None, None),
            P("section", "win", None),
            P("section", None),
            P("section", None, None, "dp"),
            P("section", "dp", None),
            P(),
            P(None, "section"),
        ),
        out_specs=P(None, "win", "dp", None, "section"),
        check_vma=False,
    )
```

```python
import functools
import math

import jax
import jax.numpy as jnp
from jax import lax
from jax.experimental import pallas as pl
from jax.experimental.pallas import tpu as pltpu
from jax.sharding import PartitionSpec as P

HEAD_DIM = 64
MESH = pl.DeviceIdType.MESH
EXCLUDED = -1e30


def normalize(hidden, scales):
    values = hidden.astype(jnp.float32)
    center = values - jnp.mean(values, axis=-1, keepdims=True)
    spread = jnp.mean(center * center, axis=-1, keepdims=True)
    return (center * lax.rsqrt(spread + 1e-05) * scales).astype(jnp.bfloat16)


def kernel(
    sections, windows, bands,
    tokens, labels, gain, wqkv_hbm, wout_hbm, final_gain, wdec_hbm,
    decoded,
    full, relay_a, relay_b, ahead, normed, projected, wqkv, wout, wdec, bias, bstage, blend, hstage, fstage, final,
    ag_send, ag_recv, a2a_send, a2a_recv, hid_send, hid_recv, fin_send, fin_recv,
    chain_send, chain_recv, fwd_send, nx_send, nx_recv, nf_send, wy_send, wy_recv, wc_send, wc_recv, load_sem,
):
    micros, quad, width = tokens.shape
    half = quad // 2
    last = sections - 1
    s = lax.axis_index("section")
    w = lax.axis_index("win")
    b = lax.axis_index("dp")
    before = lax.rem(w + windows - 1, windows)
    after = lax.rem(w + 1, windows)
    core_peer = w + 1 - 2 * lax.rem(w, 2)
    chip_peer = w + 2 - 4 * lax.rem(w // 2, 2)
    quarter = lax.rem(w, 4)
    group_rows = wout_hbm.shape[0]
    piece = group_rows // 8

    def band(k):
        return lax.rem(b + k, bands)

    def send(src, dst, send_sem, recv_sem, device):
        return pltpu.make_async_remote_copy(
            src_ref=src, dst_ref=dst, send_sem=send_sem, recv_sem=recv_sem,
            device_id=device, device_id_type=MESH,
        )

    def part_of(m, slot, part):
        return full.at[m, slot, pl.ds(half * part, half)]

    def ag_copy(m, k, part):
        slot = part_of(m, b, part)
        return send(slot, slot, ag_send.at[m, k - 1],
                    ag_recv.at[m, bands - k - 1, part], (s, w, band(k)))

    def ag_arrival(m, k, part):
        slot = part_of(m, band(k), part)
        return send(slot, slot, ag_send.at[m, k - 1], ag_recv.at[m, k - 1, part], (s, w, band(k)))

    class Chain:
        def __init__(self, index, slot, arrived):
            self.index, self.slot, self.arrived = index, slot, arrived

        def copy(self, way, distance, source):
            slot = self.slot(source)
            step = -1 if way else 1
            return send(slot, slot, chain_send.at[self.index, way, distance],
                        chain_recv.at[self.index, way, distance], (s, w, b + step))

        def each(self, distance, do):
            @pl.when((b >= distance) & (b < bands - 1))
            def _():
                do(self.copy(0, distance, b - distance))

            @pl.when((b + distance < bands) & (b > 0))
            def _():
                do(self.copy(1, distance, b + distance))

        def start(self):
            self.each(0, lambda copy: copy.start())

        def serve(self, distance):
            @pl.when(b >= distance)
            def _():
                self.copy(0, distance - 1, b - distance).wait_recv()

                if distance < bands - 1:
                    @pl.when(b < bands - 1)
                    def _():
                        self.copy(0, distance, b - distance).start()

                self.arrived(bands - distance)

            @pl.when(b + distance < bands)
            def _():
                self.copy(1, distance - 1, b + distance).wait_recv()

                if distance < bands - 1:
                    @pl.when(b > 0)
                    def _():
                        self.copy(1, distance, b + distance).start()

                self.arrived(distance)

        def drain(self):
            for distance in range(bands - 1):
                self.each(distance, lambda copy: copy.wait_send())

    def forward_copy(m, k, part):
        slot = relay_b.at[band(k), pl.ds(half * part, half)] if m else relay_a.at[band(k)]
        return send(slot, part_of(m, band(k), part), fwd_send.at[m + part if m else 0, k - 1],
                    ag_recv.at[m, k - 1, part], (0, w, b))

    def ahead_copy(m, k):
        return send(hstage.at[m, pl.ds(half, half)], ahead.at[m, b], nx_send.at[m, k - 1],
                    nx_recv.at[m, bands - k - 1], (s, w, band(k)))

    def ahead_arrival(m, k):
        slot = ahead.at[m, band(k)]
        return send(slot, slot, nx_send.at[m, k - 1], nx_recv.at[m, k - 1], (s, w, band(k)))

    def ahead_forward(m, k):
        return send(ahead.at[m, band(k)], part_of(m, band(k), 0), nf_send.at[m, k - 1],
                    ag_recv.at[m, k - 1, 0], (s + 1, w, b))

    def a2a_copy(m, k):
        return send(bstage.at[m, band(k)], blend.at[m, b], a2a_send.at[m, k - 1],
                    a2a_recv.at[m, bands - k - 1], (s, w, band(k)))

    def a2a_arrival(m, k):
        slot = blend.at[m, band(k)]
        return send(slot, slot, a2a_send.at[m, k - 1], a2a_recv.at[m, k - 1], (s, w, band(k)))

    def w_piece(slot, owner, chunk):
        start = (lax.rem(owner, 4) * 2 + chunk) * piece
        return wout.at[slot, pl.ds(pl.multiple_of(start, piece), piece)]

    def wy_copy(k, chunk):
        slot = w_piece(band(k), w, chunk)
        return send(slot, slot, wy_send.at[chunk, k - 1], wy_recv.at[chunk, k - 1], (s, chip_peer, b))

    def wy_arrival(k, chunk):
        slot = w_piece(band(k), chip_peer, chunk)
        return send(slot, slot, wy_send.at[chunk, k - 1], wy_recv.at[chunk, k - 1], (s, chip_peer, b))

    def wc_copy(k, far, chunk):
        slot = w_piece(band(k), chip_peer if far else w, chunk)
        index = 3 * far + k - 1
        return send(slot, slot, wc_send.at[chunk, index], wc_recv.at[chunk, index], (s, core_peer, b))

    def wc_arrival(k, far, chunk):
        other = core_peer + 2 - 4 * lax.rem(core_peer // 2, 2)
        slot = w_piece(band(k), other if far else core_peer, chunk)
        index = 3 * far + k - 1
        return send(slot, slot, wc_send.at[chunk, index], wc_recv.at[chunk, index], (s, core_peer, b))

    def hidden_copy(m, part):
        rows_from = pl.ds(half * (1 - part), half)
        rows_to = pl.ds(half * part, half)
        return send(hstage.at[m, rows_from], full.at[m, b, rows_to], hid_send.at[m, part],
                    hid_recv.at[m, part], (s + 1, before if part else w, b))

    def hidden_arrival(m, part):
        slot = full.at[m, b, pl.ds(half * part, half)]
        return send(slot, slot, hid_send.at[m, part], hid_recv.at[m, part], (s, after, b))

    def final_copy(m, to, part):
        rows_from = pl.ds(half * (1 - part), half)
        rows_to = pl.ds(half * part, half)
        return send(fstage.at[m, rows_from], final.at[m, rows_to], fin_send.at[m, to, part],
                    fin_recv.at[m, part], (to, before if part else w, b))

    def final_arrival(m, part):
        slot = final.at[m, pl.ds(half * part, half)]
        return send(slot, slot, fin_send.at[m, 0, part], fin_recv.at[m, part], (s, after, b))

    others = range(1, bands)
    chunks = range(2)

    def weights_arrived(chunk):
        def arrived(k):
            wy_copy(k, chunk).start()
            wc_copy(k, 0, chunk).start()
        return arrived

    def relayed(m, part):
        return lambda k: forward_copy(m, k, part).start()

    first_half = Chain(0, lambda slot: part_of(0, slot, 0), lambda k: None)
    relay_first = Chain(0, lambda slot: relay_a.at[slot], relayed(0, 1))
    weight_chains = [
        Chain(1 + c, lambda slot, c=c: w_piece(slot, w, c), weights_arrived(c)) for c in chunks
    ]
    relay_second = [
        Chain(3 + c, lambda slot, c=c: relay_b.at[slot, pl.ds(half * c, half)], relayed(1, c))
        for c in chunks
    ]

    load_qkv = pltpu.make_async_copy(wqkv_hbm, wqkv, load_sem.at[0])
    load_out = pltpu.make_async_copy(wout_hbm, wout.at[b], load_sem.at[1])
    load_dec = pltpu.make_async_copy(wdec_hbm, wdec, load_sem.at[2])
    load_qkv.start()
    load_out.start()
    load_dec.start()

    barrier = pltpu.get_barrier_semaphore()
    partners = [(s, w, band(k)) for k in others]
    partners += [(s, core_peer, b), (s, chip_peer, b)]
    partners += [(lax.rem(s + k, sections), w, b) for k in range(1, sections)]
    for to in range(sections):
        partners += [(to, before, b), (to, after, b)]
    for device in partners:
        pl.semaphore_signal(barrier, inc=1, device_id=device, device_id_type=MESH)

    @pl.when(s == 0)
    def _():
        for m in range(micros):
            full[m, b] = tokens[m]

    @pl.when(s == 1)
    def _():
        relay_a[b] = tokens[0, half:]
        relay_b[b] = tokens[1]

    pl.semaphore_wait(barrier, len(partners))

    def start_gather(m):
        hidden_arrival(m, 1).wait_recv()
        for k in others:
            ag_copy(m, k, 1).start()
        hidden_arrival(m, 0).wait_recv()

    def weights_over_cores():
        for k in others:
            for chunk in chunks:
                wy_arrival(k, chunk).wait_recv()
                wc_copy(k, 1, chunk).start()

    def weights_all():
        for k in others:
            for chunk in chunks:
                wc_arrival(k, 0, chunk).wait_recv()
                wc_arrival(k, 1, chunk).wait_recv()

    def normalize_band(m, slot):
        rows = pl.ds(pl.multiple_of(slot * quad, quad), quad)
        normed[rows, :] = normalize(full[m, slot], gain[...])

    def project(m):
        normalize_band(m, b)
        for k in others:
            if m == 0:
                @pl.when(s > 0)
                def _():
                    ag_arrival(m, k, 0).wait_recv()
            else:
                ag_arrival(m, k, 0).wait_recv()
            ag_arrival(m, k, 1).wait_recv()
            normalize_band(m, band(k))
        if m == 0:
            load_qkv.wait()
        for c in range(3):
            projected[c] = jnp.dot(
                normed[...], wqkv[c], preferred_element_type=jnp.float32
            ).astype(jnp.bfloat16)

    def attend(m):
        inner = projected.shape[2]
        rows = projected.shape[1]
        lane = lax.broadcasted_iota(jnp.int32, (rows, 128), 1)
        for pair in range(inner // 128):
            columns = slice(128 * pair, 128 * pair + 128)
            queries = projected[0, :, columns]
            keys_all = projected[1, :, columns]
            values_all = projected[2, :, columns]
            results = []
            for side in range(128 // HEAD_DIM):
                mine = (lane // HEAD_DIM) == side
                query = jnp.where(mine, queries, jnp.zeros_like(queries))
                scores = lax.dot_general(
                    query, keys_all, (((1,), (1,)), ((), ())), preferred_element_type=jnp.float32
                ) * (1.0 / math.sqrt(HEAD_DIM)) + bias[...]
                largest = jnp.max(scores, axis=-1, keepdims=True)
                weights = jnp.exp(scores - largest)
                total = jnp.sum(weights, axis=-1, keepdims=True)
                product = jnp.dot(
                    weights.astype(jnp.bfloat16), values_all, preferred_element_type=jnp.float32
                )
                results.append(product / total)
            mixed = results[0]
            for side in range(1, 128 // HEAD_DIM):
                mixed = jnp.where((lane // HEAD_DIM) == side, results[side], mixed)
            mixed = mixed.astype(jnp.bfloat16)
            for place in range(bands):
                bstage[m, place, :, columns] = mixed[place * quad:(place + 1) * quad]
        for k in others:
            a2a_copy(m, k).start()
        blend[m, b] = bstage[m, b]

    def finish(m):
        for k in others:
            a2a_arrival(m, k).wait_recv()
        for start in range(0, width, 512):
            columns = slice(start, start + 512)
            total = full[m, b, :, columns].astype(jnp.float32)
            for group in range(bands):
                total += jnp.dot(
                    blend[m, group], wout[group, :, columns], preferred_element_type=jnp.float32
                )
            hstage[m, :, columns] = total.astype(jnp.bfloat16)

        @pl.when(s < last)
        def _():
            hidden_copy(m, 1).start()
            for k in others:
                ahead_copy(m, k).start()
            hidden_copy(m, 0).start()

        @pl.when(s == last)
        def _():
            fstage[m] = normalize(hstage[m], final_gain[...].reshape(1, width))
            for to in range(sections):
                final_copy(m, to, 1).start()
                if to != last:
                    final_copy(m, to, 0).start()
            final[m, :half] = fstage[m, half:]

    def decode(m):
        @pl.when(s < last)
        def _():
            final_arrival(m, 0).wait_recv()

        final_arrival(m, 1).wait_recv()
        decoded[m] = lax.dot_general(
            final[m], wdec[...], (((1,), (1,)), ((), ())), preferred_element_type=jnp.float32
        ).astype(jnp.bfloat16)

    row = labels[...].astype(jnp.float32)
    across = jnp.broadcast_to(row, bias.shape)

    load_out.wait()

    @pl.when(s == 0)
    def _():
        for chain in [first_half, *weight_chains]:
            chain.start()

    @pl.when(s == 1)
    def _():
        relay_first.start()

    bias[...] = jnp.where(across == across.T, 0.0, EXCLUDED)

    @pl.when(s == 1)
    def _():
        relay_first.serve(1)
        relay_second[0].start()
        relay_first.serve(2)
        relay_second[1].start()
        relay_first.serve(3)
        for distance in others:
            for chain in relay_second:
                chain.serve(distance)
            if distance == 2:
                for chain in weight_chains:
                    chain.start()

    @pl.when(s > 1)
    def _():
        for chain in weight_chains:
            chain.start()

    for distance in others:
        for chain in weight_chains:
            chain.serve(distance)

        @pl.when(s == 0)
        def _():
            first_half.serve(distance)

    @pl.when(s > 0)
    def _():
        for m in range(micros):
            start_gather(m)
        weights_over_cores()

    def hand_over(m):
        @pl.when(s < last)
        def _():
            for k in others:
                ahead_arrival(m, k).wait_recv()
                ahead_forward(m, k).start()

    project(0)
    attend(0)

    @pl.when(s == 0)
    def _():
        weights_over_cores()

    weights_all()
    project(1)

    @pl.when(s < last)
    def _():
        finish(0)

    attend(1)

    @pl.when(s == last)
    def _():
        finish(0)

    hand_over(0)
    finish(1)
    hand_over(1)
    load_dec.wait()
    decode(0)
    decode(1)

    for m in range(micros):
        for k in others:
            a2a_copy(m, k).wait_send()
    for chain in weight_chains:
        chain.drain()
    for k in others:
        for chunk in chunks:
            wy_copy(k, chunk).wait_send()
            wc_copy(k, 0, chunk).wait_send()
            wc_copy(k, 1, chunk).wait_send()

    @pl.when(s == 0)
    def _():
        first_half.drain()

    @pl.when(s > 0)
    def _():
        for m in range(micros):
            for k in others:
                ag_copy(m, k, 1).wait_send()

    @pl.when(s == 1)
    def _():
        for chain in [relay_first, *relay_second]:
            chain.drain()
        for k in others:
            forward_copy(0, k, 1).wait_send()
            forward_copy(1, k, 0).wait_send()
            forward_copy(1, k, 1).wait_send()

    @pl.when(s < last)
    def _():
        for m in range(micros):
            for part in range(2):
                hidden_copy(m, part).wait_send()
            for k in others:
                ahead_copy(m, k).wait_send()
                ahead_forward(m, k).wait_send()

    @pl.when(s == last)
    def _():
        for m in range(micros):
            for to in range(sections):
                final_copy(m, to, 1).wait_send()
                if to != last:
                    final_copy(m, to, 0).wait_send()


def body(sections, windows, bands, tokens, regions, norm_gain, qkv_weight, out_weight, final_gain, dec_weight):
    micros, _, _, quad, width = tokens.shape
    inner = qkv_weight.shape[3]
    columns = dec_weight.shape[1]
    rows = bands * quad
    bf16 = jnp.bfloat16
    vmem = pl.BlockSpec(memory_space=pltpu.VMEM)
    hbm = pl.BlockSpec(memory_space=pl.ANY)
    dma = pltpu.SemaphoreType.DMA
    decoded = pl.pallas_call(
        functools.partial(kernel, sections, windows, bands),
        out_shape=jax.ShapeDtypeStruct((micros, quad, columns), bf16),
        in_specs=[vmem, vmem, vmem, hbm, hbm, vmem, hbm],
        out_specs=vmem,
        scratch_shapes=[
            pltpu.VMEM((micros, bands, quad, width), bf16),
            pltpu.VMEM((bands, quad // 2, width), bf16),
            pltpu.VMEM((bands, quad, width), bf16),
            pltpu.VMEM((micros, bands, quad // 2, width), bf16),
            pltpu.VMEM((rows, width), bf16),
            pltpu.VMEM((3, rows, inner), bf16),
            pltpu.VMEM((3, width, inner), bf16),
            pltpu.VMEM((bands, inner, width), bf16),
            pltpu.VMEM((columns, width), bf16),
            pltpu.VMEM((rows, rows), jnp.float32),
            pltpu.VMEM((micros, bands, quad, inner), bf16),
            pltpu.VMEM((micros, bands, quad, inner), bf16),
            pltpu.VMEM((micros, quad, width), bf16),
            pltpu.VMEM((micros, quad, width), bf16),
            pltpu.VMEM((micros, quad, width), bf16),
            dma((micros, 3)), dma((micros, 3, 2)),
            dma((micros, 3)), dma((micros, 3)),
            dma((micros, 2)), dma((micros, 2)),
            dma((micros, sections, 2)), dma((micros, 2)),
            dma((5, 2, 3)), dma((5, 2, 3)), dma((3, 3)),
            dma((micros, 3)), dma((micros, 3)), dma((micros, 3)),
            dma((2, 3)), dma((2, 3)),
            dma((2, 6)), dma((2, 6)),
            dma((3,)),
        ],
        compiler_params=pltpu.CompilerParams(
            collective_id=0, has_side_effects=True, vmem_limit_bytes=60 * 1024 * 1024
        ),
        name="relay",
    )(
        tokens[:, 0, 0],
        regions[0],
        norm_gain,
        jnp.transpose(qkv_weight[0], (1, 0, 2)),
        out_weight[0],
        final_gain,
        jnp.transpose(dec_weight),
    )
    return decoded[:, None, None]


def solution(mesh):
    sizes = mesh.shape
    return jax.shard_map(
        functools.partial(body, sizes["section"], sizes["win"], sizes["dp"]),
        mesh=mesh,
        in_specs=(
            P(None, "win", "dp", None, None),
            P("section", "win", None),
            P("section", None),
            P("section", None, None, "dp"),
            P("section", "dp", None),
            P(),
            P(None, "section"),
        ),
        out_specs=P(None, "win", "dp", None, "section"),
        check_vma=False,
    )
```

```python
import functools
import math

import jax
import jax.numpy as jnp
from jax import lax
from jax.experimental import pallas as pl
from jax.experimental.pallas import tpu as pltpu
from jax.sharding import PartitionSpec as P

HEAD_DIM = 64
MESH = pl.DeviceIdType.MESH
EXCLUDED = -1e30


def normalize(hidden, scales):
    values = hidden.astype(jnp.float32)
    center = values - jnp.mean(values, axis=-1, keepdims=True)
    spread = jnp.mean(center * center, axis=-1, keepdims=True)
    return (center * lax.rsqrt(spread + 1e-05) * scales).astype(jnp.bfloat16)


def kernel(
    sections, windows, bands,
    tokens, labels, gain, wqkv_hbm, wout_hbm, final_gain, wdec_hbm,
    decoded,
    full, relay_a, relay_b, ahead, normed, projected, wqkv, wout, wdec, bias, bstage, blend, hstage, fstage, final,
    ag_send, ag_recv, a2a_send, a2a_recv, hid_send, hid_recv, fin_send, fin_recv,
    chain_send, chain_recv, fwd_send, nx_send, nx_recv, nf_send, wy_send, wy_recv, wc_send, wc_recv, load_sem,
):
    micros, quad, width = tokens.shape
    half = quad // 2
    last = sections - 1
    s = lax.axis_index("section")
    w = lax.axis_index("win")
    b = lax.axis_index("dp")
    before = lax.rem(w + windows - 1, windows)
    after = lax.rem(w + 1, windows)
    core_peer = w + 1 - 2 * lax.rem(w, 2)
    chip_peer = w + 2 - 4 * lax.rem(w // 2, 2)
    quarter = lax.rem(w, 4)
    group_rows = wout_hbm.shape[0]
    piece = group_rows // 8

    def band(k):
        return lax.rem(b + k, bands)

    def send(src, dst, send_sem, recv_sem, device):
        return pltpu.make_async_remote_copy(
            src_ref=src, dst_ref=dst, send_sem=send_sem, recv_sem=recv_sem,
            device_id=device, device_id_type=MESH,
        )

    def part_of(m, slot, part):
        return full.at[m, slot, pl.ds(half * part, half)]

    def ag_copy(m, k, part):
        slot = part_of(m, b, part)
        return send(slot, slot, ag_send.at[m, k - 1],
                    ag_recv.at[m, bands - k - 1, part], (s, w, band(k)))

    def ag_arrival(m, k, part):
        slot = part_of(m, band(k), part)
        return send(slot, slot, ag_send.at[m, k - 1], ag_recv.at[m, k - 1, part], (s, w, band(k)))

    class Chain:
        def __init__(self, index, slot, arrived):
            self.index, self.slot, self.arrived = index, slot, arrived

        def copy(self, way, distance, source):
            slot = self.slot(source)
            step = -1 if way else 1
            return send(slot, slot, chain_send.at[self.index, way, distance],
                        chain_recv.at[self.index, way, distance], (s, w, b + step))

        def each(self, distance, do):
            @pl.when((b >= distance) & (b < bands - 1))
            def _():
                do(self.copy(0, distance, b - distance))

            @pl.when((b + distance < bands) & (b > 0))
            def _():
                do(self.copy(1, distance, b + distance))

        def start(self):
            self.each(0, lambda copy: copy.start())

        def serve(self, distance):
            @pl.when(b >= distance)
            def _():
                self.copy(0, distance - 1, b - distance).wait_recv()

                if distance < bands - 1:
                    @pl.when(b < bands - 1)
                    def _():
                        self.copy(0, distance, b - distance).start()

                self.arrived(bands - distance)

            @pl.when(b + distance < bands)
            def _():
                self.copy(1, distance - 1, b + distance).wait_recv()

                if distance < bands - 1:
                    @pl.when(b > 0)
                    def _():
                        self.copy(1, distance, b + distance).start()

                self.arrived(distance)

        def drain(self):
            for distance in range(bands - 1):
                self.each(distance, lambda copy: copy.wait_send())

    def forward_copy(m, k):
        slot = (relay_b if m else relay_a).at[band(k)]
        return send(slot, part_of(m, band(k), 1), fwd_send.at[m, k - 1],
                    ag_recv.at[m, k - 1, 1], (0, w, b))

    def ahead_copy(m, k):
        return send(hstage.at[m, pl.ds(half, half)], ahead.at[m, b], nx_send.at[m, k - 1],
                    nx_recv.at[m, bands - k - 1], (s, w, band(k)))

    def ahead_arrival(m, k):
        slot = ahead.at[m, band(k)]
        return send(slot, slot, nx_send.at[m, k - 1], nx_recv.at[m, k - 1], (s, w, band(k)))

    def ahead_forward(m, k):
        return send(ahead.at[m, band(k)], part_of(m, band(k), 0), nf_send.at[m, k - 1],
                    ag_recv.at[m, k - 1, 0], (s + 1, w, b))

    def a2a_copy(m, k):
        return send(bstage.at[m, band(k)], blend.at[m, b], a2a_send.at[m, k - 1],
                    a2a_recv.at[m, bands - k - 1], (s, w, band(k)))

    def a2a_arrival(m, k):
        slot = blend.at[m, band(k)]
        return send(slot, slot, a2a_send.at[m, k - 1], a2a_recv.at[m, k - 1], (s, w, band(k)))

    def w_piece(slot, owner, chunk):
        start = (lax.rem(owner, 4) * 2 + chunk) * piece
        return wout.at[slot, pl.ds(pl.multiple_of(start, piece), piece)]

    def wy_copy(k, chunk):
        slot = w_piece(band(k), w, chunk)
        return send(slot, slot, wy_send.at[chunk, k - 1], wy_recv.at[chunk, k - 1], (s, chip_peer, b))

    def wy_arrival(k, chunk):
        slot = w_piece(band(k), chip_peer, chunk)
        return send(slot, slot, wy_send.at[chunk, k - 1], wy_recv.at[chunk, k - 1], (s, chip_peer, b))

    def wc_copy(k, far, chunk):
        slot = w_piece(band(k), chip_peer if far else w, chunk)
        index = 3 * far + k - 1
        return send(slot, slot, wc_send.at[chunk, index], wc_recv.at[chunk, index], (s, core_peer, b))

    def wc_arrival(k, far, chunk):
        other = core_peer + 2 - 4 * lax.rem(core_peer // 2, 2)
        slot = w_piece(band(k), other if far else core_peer, chunk)
        index = 3 * far + k - 1
        return send(slot, slot, wc_send.at[chunk, index], wc_recv.at[chunk, index], (s, core_peer, b))

    def hidden_copy(m, part):
        rows_from = pl.ds(half * (1 - part), half)
        rows_to = pl.ds(half * part, half)
        return send(hstage.at[m, rows_from], full.at[m, b, rows_to], hid_send.at[m, part],
                    hid_recv.at[m, part], (s + 1, before if part else w, b))

    def hidden_arrival(m, part):
        slot = full.at[m, b, pl.ds(half * part, half)]
        return send(slot, slot, hid_send.at[m, part], hid_recv.at[m, part], (s, after, b))

    def final_copy(m, to, part):
        rows_from = pl.ds(half * (1 - part), half)
        rows_to = pl.ds(half * part, half)
        return send(fstage.at[m, rows_from], final.at[m, rows_to], fin_send.at[m, to, part],
                    fin_recv.at[m, part], (to, before if part else w, b))

    def final_arrival(m, part):
        slot = final.at[m, pl.ds(half * part, half)]
        return send(slot, slot, fin_send.at[m, 0, part], fin_recv.at[m, part], (s, after, b))

    others = range(1, bands)
    chunks = range(2)

    def weights_arrived(chunk):
        def arrived(k):
            wy_copy(k, chunk).start()
            wc_copy(k, 0, chunk).start()
        return arrived

    def relayed(m):
        return lambda k: forward_copy(m, k).start()

    own_halves = [
        Chain(3 * m, lambda slot, m=m: part_of(m, slot, 0), lambda k: None) for m in range(2)
    ]
    relays = [
        Chain(0, lambda slot: relay_a.at[slot], relayed(0)),
        Chain(3, lambda slot: relay_b.at[slot], relayed(1)),
    ]
    weight_chains = [
        Chain(1 + c, lambda slot, c=c: w_piece(slot, w, c), weights_arrived(c)) for c in chunks
    ]

    load_qkv = pltpu.make_async_copy(wqkv_hbm, wqkv, load_sem.at[0])
    load_out = pltpu.make_async_copy(wout_hbm, wout.at[b], load_sem.at[1])
    load_dec = pltpu.make_async_copy(wdec_hbm, wdec, load_sem.at[2])
    load_qkv.start()
    load_out.start()
    load_dec.start()

    barrier = pltpu.get_barrier_semaphore()
    partners = [(s, w, band(k)) for k in others]
    partners += [(s, core_peer, b), (s, chip_peer, b)]
    partners += [(lax.rem(s + k, sections), w, b) for k in range(1, sections)]
    for to in range(sections):
        partners += [(to, before, b), (to, after, b)]
    for device in partners:
        pl.semaphore_signal(barrier, inc=1, device_id=device, device_id_type=MESH)

    @pl.when(s == 0)
    def _():
        for m in range(micros):
            full[m, b] = tokens[m]

    @pl.when(s == 1)
    def _():
        relay_a[b] = tokens[0, half:]
        relay_b[b] = tokens[1, half:]

    pl.semaphore_wait(barrier, len(partners))

    def start_gather(m):
        hidden_arrival(m, 1).wait_recv()
        for k in others:
            ag_copy(m, k, 1).start()
        hidden_arrival(m, 0).wait_recv()

    def weights_over_cores():
        for k in others:
            for chunk in chunks:
                wy_arrival(k, chunk).wait_recv()
                wc_copy(k, 1, chunk).start()

    def weights_all():
        for k in others:
            for chunk in chunks:
                wc_arrival(k, 0, chunk).wait_recv()
                wc_arrival(k, 1, chunk).wait_recv()

    def normalize_band(m, slot):
        rows = pl.ds(pl.multiple_of(slot * quad, quad), quad)
        normed[rows, :] = normalize(full[m, slot], gain[...])

    def project(m):
        normalize_band(m, b)
        for k in others:
            @pl.when(s > 0)
            def _():
                ag_arrival(m, k, 0).wait_recv()

            ag_arrival(m, k, 1).wait_recv()
            normalize_band(m, band(k))
        if m == 0:
            load_qkv.wait()
        for c in range(3):
            projected[c] = jnp.dot(
                normed[...], wqkv[c], preferred_element_type=jnp.float32
            ).astype(jnp.bfloat16)

    def attend(m):
        inner = projected.shape[2]
        rows = projected.shape[1]
        lane = lax.broadcasted_iota(jnp.int32, (rows, 128), 1)
        for pair in range(inner // 128):
            columns = slice(128 * pair, 128 * pair + 128)
            queries = projected[0, :, columns]
            keys_all = projected[1, :, columns]
            values_all = projected[2, :, columns]
            results = []
            for side in range(128 // HEAD_DIM):
                mine = (lane // HEAD_DIM) == side
                query = jnp.where(mine, queries, jnp.zeros_like(queries))
                scores = lax.dot_general(
                    query, keys_all, (((1,), (1,)), ((), ())), preferred_element_type=jnp.float32
                ) * (1.0 / math.sqrt(HEAD_DIM)) + bias[...]
                largest = jnp.max(scores, axis=-1, keepdims=True)
                weights = jnp.exp(scores - largest)
                total = jnp.sum(weights, axis=-1, keepdims=True)
                product = jnp.dot(
                    weights.astype(jnp.bfloat16), values_all, preferred_element_type=jnp.float32
                )
                results.append(product / total)
            mixed = results[0]
            for side in range(1, 128 // HEAD_DIM):
                mixed = jnp.where((lane // HEAD_DIM) == side, results[side], mixed)
            mixed = mixed.astype(jnp.bfloat16)
            for place in range(bands):
                bstage[m, place, :, columns] = mixed[place * quad:(place + 1) * quad]
        for k in others:
            a2a_copy(m, k).start()
        blend[m, b] = bstage[m, b]

    def finish(m):
        for k in others:
            a2a_arrival(m, k).wait_recv()
        for start in range(0, width, 512):
            columns = slice(start, start + 512)
            total = full[m, b, :, columns].astype(jnp.float32)
            for group in range(bands):
                total += jnp.dot(
                    blend[m, group], wout[group, :, columns], preferred_element_type=jnp.float32
                )
            hstage[m, :, columns] = total.astype(jnp.bfloat16)

        @pl.when(s < last)
        def _():
            hidden_copy(m, 1).start()
            for k in others:
                ahead_copy(m, k).start()
            hidden_copy(m, 0).start()

        @pl.when(s == last)
        def _():
            fstage[m] = normalize(hstage[m], final_gain[...].reshape(1, width))
            for to in range(sections):
                final_copy(m, to, 1).start()
                if to != last:
                    final_copy(m, to, 0).start()
            final[m, :half] = fstage[m, half:]

    def decode(m):
        @pl.when(s < last)
        def _():
            final_arrival(m, 0).wait_recv()

        final_arrival(m, 1).wait_recv()
        decoded[m] = lax.dot_general(
            final[m], wdec[...], (((1,), (1,)), ((), ())), preferred_element_type=jnp.float32
        ).astype(jnp.bfloat16)

    row = labels[...].astype(jnp.float32)
    across = jnp.broadcast_to(row, bias.shape)

    load_out.wait()

    @pl.when(s == 0)
    def _():
        for chain in [own_halves[0], *weight_chains]:
            chain.start()

    @pl.when(s == 1)
    def _():
        for chain in relays:
            chain.start()

    bias[...] = jnp.where(across == across.T, 0.0, EXCLUDED)

    @pl.when(s == 1)
    def _():
        for distance in others:
            for chain in relays:
                chain.serve(distance)
            if distance == 2:
                for chain in weight_chains:
                    chain.start()

    @pl.when(s > 1)
    def _():
        for chain in weight_chains:
            chain.start()

    for distance in others:
        for chain in weight_chains:
            chain.serve(distance)

        @pl.when(s == 0)
        def _():
            own_halves[0].serve(distance)
            if distance == 2:
                own_halves[1].start()

    @pl.when(s > 0)
    def _():
        for m in range(micros):
            start_gather(m)
        weights_over_cores()

    def hand_over(m):
        @pl.when(s < last)
        def _():
            for k in others:
                ahead_arrival(m, k).wait_recv()
                ahead_forward(m, k).start()

    project(0)

    @pl.when(s == 0)
    def _():
        own_halves[1].serve(1)

    attend(0)

    @pl.when(s == 0)
    def _():
        own_halves[1].serve(2)
        weights_over_cores()
        own_halves[1].serve(3)

    weights_all()
    project(1)

    @pl.when(s < last)
    def _():
        finish(0)

    attend(1)

    @pl.when(s == last)
    def _():
        finish(0)

    hand_over(0)
    finish(1)
    hand_over(1)
    load_dec.wait()
    decode(0)
    decode(1)

    for m in range(micros):
        for k in others:
            a2a_copy(m, k).wait_send()
    for chain in weight_chains:
        chain.drain()
    for k in others:
        for chunk in chunks:
            wy_copy(k, chunk).wait_send()
            wc_copy(k, 0, chunk).wait_send()
            wc_copy(k, 1, chunk).wait_send()

    @pl.when(s == 0)
    def _():
        for chain in own_halves:
            chain.drain()

    @pl.when(s > 0)
    def _():
        for m in range(micros):
            for k in others:
                ag_copy(m, k, 1).wait_send()

    @pl.when(s == 1)
    def _():
        for chain in relays:
            chain.drain()
        for k in others:
            forward_copy(0, k).wait_send()
            forward_copy(1, k).wait_send()

    @pl.when(s < last)
    def _():
        for m in range(micros):
            for part in range(2):
                hidden_copy(m, part).wait_send()
            for k in others:
                ahead_copy(m, k).wait_send()
                ahead_forward(m, k).wait_send()

    @pl.when(s == last)
    def _():
        for m in range(micros):
            for to in range(sections):
                final_copy(m, to, 1).wait_send()
                if to != last:
                    final_copy(m, to, 0).wait_send()


def body(sections, windows, bands, tokens, regions, norm_gain, qkv_weight, out_weight, final_gain, dec_weight):
    micros, _, _, quad, width = tokens.shape
    inner = qkv_weight.shape[3]
    columns = dec_weight.shape[1]
    rows = bands * quad
    bf16 = jnp.bfloat16
    vmem = pl.BlockSpec(memory_space=pltpu.VMEM)
    hbm = pl.BlockSpec(memory_space=pl.ANY)
    dma = pltpu.SemaphoreType.DMA
    decoded = pl.pallas_call(
        functools.partial(kernel, sections, windows, bands),
        out_shape=jax.ShapeDtypeStruct((micros, quad, columns), bf16),
        in_specs=[vmem, vmem, vmem, hbm, hbm, vmem, hbm],
        out_specs=vmem,
        scratch_shapes=[
            pltpu.VMEM((micros, bands, quad, width), bf16),
            pltpu.VMEM((bands, quad // 2, width), bf16),
            pltpu.VMEM((bands, quad // 2, width), bf16),
            pltpu.VMEM((micros, bands, quad // 2, width), bf16),
            pltpu.VMEM((rows, width), bf16),
            pltpu.VMEM((3, rows, inner), bf16),
            pltpu.VMEM((3, width, inner), bf16),
            pltpu.VMEM((bands, inner, width), bf16),
            pltpu.VMEM((columns, width), bf16),
            pltpu.VMEM((rows, rows), jnp.float32),
            pltpu.VMEM((micros, bands, quad, inner), bf16),
            pltpu.VMEM((micros, bands, quad, inner), bf16),
            pltpu.VMEM((micros, quad, width), bf16),
            pltpu.VMEM((micros, quad, width), bf16),
            pltpu.VMEM((micros, quad, width), bf16),
            dma((micros, 3)), dma((micros, 3, 2)),
            dma((micros, 3)), dma((micros, 3)),
            dma((micros, 2)), dma((micros, 2)),
            dma((micros, sections, 2)), dma((micros, 2)),
            dma((4, 2, 3)), dma((4, 2, 3)), dma((2, 3)),
            dma((micros, 3)), dma((micros, 3)), dma((micros, 3)),
            dma((2, 3)), dma((2, 3)),
            dma((2, 6)), dma((2, 6)),
            dma((3,)),
        ],
        compiler_params=pltpu.CompilerParams(
            collective_id=0, has_side_effects=True, vmem_limit_bytes=60 * 1024 * 1024
        ),
        name="relay",
    )(
        tokens[:, 0, 0],
        regions[0],
        norm_gain,
        jnp.transpose(qkv_weight[0], (1, 0, 2)),
        out_weight[0],
        final_gain,
        jnp.transpose(dec_weight),
    )
    return decoded[:, None, None]


def solution(mesh):
    sizes = mesh.shape
    return jax.shard_map(
        functools.partial(body, sizes["section"], sizes["win"], sizes["dp"]),
        mesh=mesh,
        in_specs=(
            P(None, "win", "dp", None, None),
            P("section", "win", None),
            P("section", None),
            P("section", None, None, "dp"),
            P("section", "dp", None),
            P(),
            P(None, "section"),
        ),
        out_specs=P(None, "win", "dp", None, "section"),
        check_vma=False,
    )
```

```python
import functools
import math

import jax
import jax.numpy as jnp
from jax import lax
from jax.experimental import pallas as pl
from jax.experimental.pallas import tpu as pltpu
from jax.sharding import PartitionSpec as P

HEAD_DIM = 64
MESH = pl.DeviceIdType.MESH
EXCLUDED = -1e30


def normalize(hidden, scales):
    values = hidden.astype(jnp.float32)
    center = values - jnp.mean(values, axis=-1, keepdims=True)
    spread = jnp.mean(center * center, axis=-1, keepdims=True)
    return (center * lax.rsqrt(spread + 1e-05) * scales).astype(jnp.bfloat16)


def kernel(
    sections, windows, bands,
    tokens, labels, gain, wqkv_hbm, wout_hbm, final_gain, wdec_hbm,
    decoded,
    full, relay_a, relay_b, ahead, normed, projected, wqkv, wout, wdec, bias, bstage, blend, hstage, fstage, final,
    ag_send, ag_recv, a2a_send, a2a_recv, hid_send, hid_recv, fin_send, fin_recv,
    chain_send, chain_recv, fwd_send, nx_send, nx_recv, nf_send, wy_send, wy_recv, wc_send, wc_recv, load_sem,
):
    micros, quad, width = tokens.shape
    half = quad // 2
    last = sections - 1
    s = lax.axis_index("section")
    w = lax.axis_index("win")
    b = lax.axis_index("dp")
    before = lax.rem(w + windows - 1, windows)
    after = lax.rem(w + 1, windows)
    core_peer = w + 1 - 2 * lax.rem(w, 2)
    chip_peer = w + 2 - 4 * lax.rem(w // 2, 2)
    quarter = lax.rem(w, 4)
    group_rows = wout_hbm.shape[0]
    piece = group_rows // 8

    def band(k):
        return lax.rem(b + k, bands)

    def send(src, dst, send_sem, recv_sem, device):
        return pltpu.make_async_remote_copy(
            src_ref=src, dst_ref=dst, send_sem=send_sem, recv_sem=recv_sem,
            device_id=device, device_id_type=MESH,
        )

    def part_of(m, slot, part):
        return full.at[m, slot, pl.ds(half * part, half)]

    def ag_copy(m, k, part):
        slot = part_of(m, b, part)
        return send(slot, slot, ag_send.at[m, k - 1],
                    ag_recv.at[m, bands - k - 1, part], (s, w, band(k)))

    def ag_arrival(m, k, part):
        slot = part_of(m, band(k), part)
        return send(slot, slot, ag_send.at[m, k - 1], ag_recv.at[m, k - 1, part], (s, w, band(k)))

    class Chain:
        def __init__(self, index, slot, arrived):
            self.index, self.slot, self.arrived = index, slot, arrived

        def copy(self, way, distance, source):
            slot = self.slot(source)
            step = -1 if way else 1
            return send(slot, slot, chain_send.at[self.index, way, distance],
                        chain_recv.at[self.index, way, distance], (s, w, b + step))

        def each(self, distance, do):
            @pl.when((b >= distance) & (b < bands - 1))
            def _():
                do(self.copy(0, distance, b - distance))

            @pl.when((b + distance < bands) & (b > 0))
            def _():
                do(self.copy(1, distance, b + distance))

        def start(self):
            self.each(0, lambda copy: copy.start())

        def serve(self, distance):
            @pl.when(b >= distance)
            def _():
                self.copy(0, distance - 1, b - distance).wait_recv()

                if distance < bands - 1:
                    @pl.when(b < bands - 1)
                    def _():
                        self.copy(0, distance, b - distance).start()

                self.arrived(bands - distance)

            @pl.when(b + distance < bands)
            def _():
                self.copy(1, distance - 1, b + distance).wait_recv()

                if distance < bands - 1:
                    @pl.when(b > 0)
                    def _():
                        self.copy(1, distance, b + distance).start()

                self.arrived(distance)

        def drain(self):
            for distance in range(bands - 1):
                self.each(distance, lambda copy: copy.wait_send())

    def forward_copy(m, k, part):
        slot = relay_b.at[band(k), pl.ds(half * part, half)] if m else relay_a.at[band(k)]
        return send(slot, part_of(m, band(k), part), fwd_send.at[m + part if m else 0, k - 1],
                    ag_recv.at[m, k - 1, part], (0, w, b))

    def ahead_copy(m, k):
        return send(hstage.at[m, pl.ds(half, half)], ahead.at[m, b], nx_send.at[m, k - 1],
                    nx_recv.at[m, bands - k - 1], (s, w, band(k)))

    def ahead_arrival(m, k):
        slot = ahead.at[m, band(k)]
        return send(slot, slot, nx_send.at[m, k - 1], nx_recv.at[m, k - 1], (s, w, band(k)))

    def ahead_forward(m, k):
        return send(ahead.at[m, band(k)], part_of(m, band(k), 0), nf_send.at[m, k - 1],
                    ag_recv.at[m, k - 1, 0], (s + 1, w, b))

    pairs = range(wqkv.shape[2] // 128)

    def a2a_copy(m, k, pair):
        columns = pl.ds(128 * pair, 128)
        return send(bstage.at[m, band(k), :, columns], blend.at[m, b, :, columns],
                    a2a_send.at[m, k - 1, pair], a2a_recv.at[m, bands - k - 1, pair], (s, w, band(k)))

    def a2a_arrival(m, k, pair):
        slot = blend.at[m, band(k), :, pl.ds(128 * pair, 128)]
        return send(slot, slot, a2a_send.at[m, k - 1, pair], a2a_recv.at[m, k - 1, pair],
                    (s, w, band(k)))

    def w_piece(slot, owner, chunk):
        start = (lax.rem(owner, 4) * 2 + chunk) * piece
        return wout.at[slot, pl.ds(pl.multiple_of(start, piece), piece)]

    def wy_copy(k, chunk):
        slot = w_piece(band(k), w, chunk)
        return send(slot, slot, wy_send.at[chunk, k - 1], wy_recv.at[chunk, k - 1], (s, chip_peer, b))

    def wy_arrival(k, chunk):
        slot = w_piece(band(k), chip_peer, chunk)
        return send(slot, slot, wy_send.at[chunk, k - 1], wy_recv.at[chunk, k - 1], (s, chip_peer, b))

    def wc_copy(k, far, chunk):
        slot = w_piece(band(k), chip_peer if far else w, chunk)
        index = 3 * far + k - 1
        return send(slot, slot, wc_send.at[chunk, index], wc_recv.at[chunk, index], (s, core_peer, b))

    def wc_arrival(k, far, chunk):
        other = core_peer + 2 - 4 * lax.rem(core_peer // 2, 2)
        slot = w_piece(band(k), other if far else core_peer, chunk)
        index = 3 * far + k - 1
        return send(slot, slot, wc_send.at[chunk, index], wc_recv.at[chunk, index], (s, core_peer, b))

    def hidden_copy(m, part):
        rows_from = pl.ds(half * (1 - part), half)
        rows_to = pl.ds(half * part, half)
        return send(hstage.at[m, rows_from], full.at[m, b, rows_to], hid_send.at[m, part],
                    hid_recv.at[m, part], (s + 1, before if part else w, b))

    def hidden_arrival(m, part):
        slot = full.at[m, b, pl.ds(half * part, half)]
        return send(slot, slot, hid_send.at[m, part], hid_recv.at[m, part], (s, after, b))

    def final_copy(m, to, part):
        rows_from = pl.ds(half * (1 - part), half)
        rows_to = pl.ds(half * part, half)
        return send(fstage.at[m, rows_from], final.at[m, rows_to], fin_send.at[m, to, part],
                    fin_recv.at[m, part], (to, before if part else w, b))

    def final_arrival(m, part):
        slot = final.at[m, pl.ds(half * part, half)]
        return send(slot, slot, fin_send.at[m, 0, part], fin_recv.at[m, part], (s, after, b))

    others = range(1, bands)
    chunks = range(2)

    def weights_arrived(chunk):
        def arrived(k):
            wy_copy(k, chunk).start()
            wc_copy(k, 0, chunk).start()
        return arrived

    def relayed(m, part):
        return lambda k: forward_copy(m, k, part).start()

    first_half = Chain(0, lambda slot: part_of(0, slot, 0), lambda k: None)
    relay_first = Chain(0, lambda slot: relay_a.at[slot], relayed(0, 1))
    weight_chains = [
        Chain(1 + c, lambda slot, c=c: w_piece(slot, w, c), weights_arrived(c)) for c in chunks
    ]
    relay_second = [
        Chain(3 + c, lambda slot, c=c: relay_b.at[slot, pl.ds(half * c, half)], relayed(1, c))
        for c in chunks
    ]

    load_qkv = pltpu.make_async_copy(wqkv_hbm, wqkv, load_sem.at[0])
    load_out = pltpu.make_async_copy(wout_hbm, wout.at[b], load_sem.at[1])
    load_dec = pltpu.make_async_copy(wdec_hbm, wdec, load_sem.at[2])
    load_qkv.start()
    load_out.start()
    load_dec.start()

    barrier = pltpu.get_barrier_semaphore()
    partners = [(s, w, band(k)) for k in others]
    partners += [(s, core_peer, b), (s, chip_peer, b)]
    partners += [(lax.rem(s + k, sections), w, b) for k in range(1, sections)]
    for to in range(sections):
        partners += [(to, before, b), (to, after, b)]
    for device in partners:
        pl.semaphore_signal(barrier, inc=1, device_id=device, device_id_type=MESH)

    @pl.when(s == 0)
    def _():
        for m in range(micros):
            full[m, b] = tokens[m]

    @pl.when(s == 1)
    def _():
        relay_a[b] = tokens[0, half:]
        relay_b[b] = tokens[1]

    pl.semaphore_wait(barrier, len(partners))

    def start_gather(m):
        hidden_arrival(m, 1).wait_recv()
        for k in others:
            ag_copy(m, k, 1).start()
        hidden_arrival(m, 0).wait_recv()

    def weights_over_cores():
        for k in others:
            for chunk in chunks:
                wy_arrival(k, chunk).wait_recv()
                wc_copy(k, 1, chunk).start()

    def weights_all():
        for k in others:
            for chunk in chunks:
                wc_arrival(k, 0, chunk).wait_recv()
                wc_arrival(k, 1, chunk).wait_recv()

    def normalize_band(m, slot):
        rows = pl.ds(pl.multiple_of(slot * quad, quad), quad)
        normed[rows, :] = normalize(full[m, slot], gain[...])

    def project(m):
        normalize_band(m, b)
        for k in others:
            if m == 0:
                @pl.when(s > 0)
                def _():
                    ag_arrival(m, k, 0).wait_recv()
            else:
                ag_arrival(m, k, 0).wait_recv()
            ag_arrival(m, k, 1).wait_recv()
            normalize_band(m, band(k))
        if m == 0:
            load_qkv.wait()
        for c in range(3):
            projected[c] = jnp.dot(
                normed[...], wqkv[c], preferred_element_type=jnp.float32
            ).astype(jnp.bfloat16)

    def attend(m):
        rows = projected.shape[1]
        lane = lax.broadcasted_iota(jnp.int32, (rows, 128), 1)
        for pair in pairs:
            columns = slice(128 * pair, 128 * pair + 128)
            queries = projected[0, :, columns] * (1.0 / math.sqrt(HEAD_DIM))
            keys_all = projected[1, :, columns]
            values_all = projected[2, :, columns]
            results = []
            for side in range(128 // HEAD_DIM):
                mine = (lane // HEAD_DIM) == side
                query = jnp.where(mine, queries, jnp.zeros_like(queries))
                scores = lax.dot_general(
                    query, keys_all, (((1,), (1,)), ((), ())), preferred_element_type=jnp.float32
                ) + bias[...]
                largest = jnp.max(scores, axis=-1, keepdims=True)
                weights = jnp.exp(scores - largest)
                total = jnp.sum(weights, axis=-1, keepdims=True)
                product = jnp.dot(
                    weights.astype(jnp.bfloat16), values_all, preferred_element_type=jnp.float32
                )
                results.append(product / total)
            mixed = results[0]
            for side in range(1, 128 // HEAD_DIM):
                mixed = jnp.where((lane // HEAD_DIM) == side, results[side], mixed)
            mixed = mixed.astype(jnp.bfloat16)
            for place in range(bands):
                bstage[m, place, :, columns] = mixed[place * quad:(place + 1) * quad]
            for k in others:
                a2a_copy(m, k, pair).start()
            blend[m, b, :, columns] = bstage[m, b, :, columns]

    def finish(m):
        for k in others:
            for pair in pairs:
                a2a_arrival(m, k, pair).wait_recv()
        for start in range(0, width, 512):
            columns = slice(start, start + 512)
            total = full[m, b, :, columns].astype(jnp.float32)
            for group in range(bands):
                total += jnp.dot(
                    blend[m, group], wout[group, :, columns], preferred_element_type=jnp.float32
                )
            hstage[m, :, columns] = total.astype(jnp.bfloat16)

        @pl.when(s < last)
        def _():
            hidden_copy(m, 1).start()
            for k in others:
                ahead_copy(m, k).start()
            hidden_copy(m, 0).start()

        @pl.when(s == last)
        def _():
            fstage[m] = normalize(hstage[m], final_gain[...].reshape(1, width))
            for to in range(sections):
                final_copy(m, to, 1).start()
                if to != last:
                    final_copy(m, to, 0).start()
            final[m, :half] = fstage[m, half:]

    def decode(m):
        @pl.when(s < last)
        def _():
            final_arrival(m, 0).wait_recv()

        final_arrival(m, 1).wait_recv()
        decoded[m] = lax.dot_general(
            final[m], wdec[...], (((1,), (1,)), ((), ())), preferred_element_type=jnp.float32
        ).astype(jnp.bfloat16)

    row = labels[...].astype(jnp.float32)
    across = jnp.broadcast_to(row, bias.shape)

    load_out.wait()

    @pl.when(s == 0)
    def _():
        for chain in [first_half, *weight_chains]:
            chain.start()

    @pl.when(s == 1)
    def _():
        relay_first.start()

    bias[...] = jnp.where(across == across.T, 0.0, EXCLUDED)

    @pl.when(s == 1)
    def _():
        relay_first.serve(1)
        relay_second[0].start()
        relay_first.serve(2)
        relay_second[1].start()
        relay_first.serve(3)
        for distance in others:
            for chain in relay_second:
                chain.serve(distance)
            if distance == 2:
                for chain in weight_chains:
                    chain.start()

    @pl.when(s > 1)
    def _():
        for chain in weight_chains:
            chain.start()

    for distance in others:
        for chain in weight_chains:
            chain.serve(distance)

        @pl.when(s == 0)
        def _():
            first_half.serve(distance)

    @pl.when(s > 0)
    def _():
        for m in range(micros):
            start_gather(m)
        weights_over_cores()

    def hand_over(m):
        @pl.when(s < last)
        def _():
            for k in others:
                ahead_arrival(m, k).wait_recv()
                ahead_forward(m, k).start()

    project(0)
    attend(0)

    @pl.when(s == 0)
    def _():
        weights_over_cores()

    weights_all()
    project(1)

    @pl.when(s < last)
    def _():
        finish(0)

    attend(1)

    @pl.when(s == last)
    def _():
        finish(0)

    hand_over(0)
    finish(1)
    hand_over(1)
    load_dec.wait()
    decode(0)
    decode(1)

    for m in range(micros):
        for k in others:
            for pair in pairs:
                a2a_copy(m, k, pair).wait_send()
    for chain in weight_chains:
        chain.drain()
    for k in others:
        for chunk in chunks:
            wy_copy(k, chunk).wait_send()
            wc_copy(k, 0, chunk).wait_send()
            wc_copy(k, 1, chunk).wait_send()

    @pl.when(s == 0)
    def _():
        first_half.drain()

    @pl.when(s > 0)
    def _():
        for m in range(micros):
            for k in others:
                ag_copy(m, k, 1).wait_send()

    @pl.when(s == 1)
    def _():
        for chain in [relay_first, *relay_second]:
            chain.drain()
        for k in others:
            forward_copy(0, k, 1).wait_send()
            forward_copy(1, k, 0).wait_send()
            forward_copy(1, k, 1).wait_send()

    @pl.when(s < last)
    def _():
        for m in range(micros):
            for part in range(2):
                hidden_copy(m, part).wait_send()
            for k in others:
                ahead_copy(m, k).wait_send()
                ahead_forward(m, k).wait_send()

    @pl.when(s == last)
    def _():
        for m in range(micros):
            for to in range(sections):
                final_copy(m, to, 1).wait_send()
                if to != last:
                    final_copy(m, to, 0).wait_send()


def body(sections, windows, bands, tokens, regions, norm_gain, qkv_weight, out_weight, final_gain, dec_weight):
    micros, _, _, quad, width = tokens.shape
    inner = qkv_weight.shape[3]
    columns = dec_weight.shape[1]
    rows = bands * quad
    bf16 = jnp.bfloat16
    vmem = pl.BlockSpec(memory_space=pltpu.VMEM)
    hbm = pl.BlockSpec(memory_space=pl.ANY)
    dma = pltpu.SemaphoreType.DMA
    decoded = pl.pallas_call(
        functools.partial(kernel, sections, windows, bands),
        out_shape=jax.ShapeDtypeStruct((micros, quad, columns), bf16),
        in_specs=[vmem, vmem, vmem, hbm, hbm, vmem, hbm],
        out_specs=vmem,
        scratch_shapes=[
            pltpu.VMEM((micros, bands, quad, width), bf16),
            pltpu.VMEM((bands, quad // 2, width), bf16),
            pltpu.VMEM((bands, quad, width), bf16),
            pltpu.VMEM((micros, bands, quad // 2, width), bf16),
            pltpu.VMEM((rows, width), bf16),
            pltpu.VMEM((3, rows, inner), bf16),
            pltpu.VMEM((3, width, inner), bf16),
            pltpu.VMEM((bands, inner, width), bf16),
            pltpu.VMEM((columns, width), bf16),
            pltpu.VMEM((rows, rows), jnp.float32),
            pltpu.VMEM((micros, bands, quad, inner), bf16),
            pltpu.VMEM((micros, bands, quad, inner), bf16),
            pltpu.VMEM((micros, quad, width), bf16),
            pltpu.VMEM((micros, quad, width), bf16),
            pltpu.VMEM((micros, quad, width), bf16),
            dma((micros, 3)), dma((micros, 3, 2)),
            dma((micros, 3, inner // 128)), dma((micros, 3, inner // 128)),
            dma((micros, 2)), dma((micros, 2)),
            dma((micros, sections, 2)), dma((micros, 2)),
            dma((5, 2, 3)), dma((5, 2, 3)), dma((3, 3)),
            dma((micros, 3)), dma((micros, 3)), dma((micros, 3)),
            dma((2, 3)), dma((2, 3)),
            dma((2, 6)), dma((2, 6)),
            dma((3,)),
        ],
        compiler_params=pltpu.CompilerParams(
            collective_id=0, has_side_effects=True, vmem_limit_bytes=60 * 1024 * 1024
        ),
        name="relay",
    )(
        tokens[:, 0, 0],
        regions[0],
        norm_gain,
        jnp.transpose(qkv_weight[0], (1, 0, 2)),
        out_weight[0],
        final_gain,
        jnp.transpose(dec_weight),
    )
    return decoded[:, None, None]


def solution(mesh):
    sizes = mesh.shape
    return jax.shard_map(
        functools.partial(body, sizes["section"], sizes["win"], sizes["dp"]),
        mesh=mesh,
        in_specs=(
            P(None, "win", "dp", None, None),
            P("section", "win", None),
            P("section", None),
            P("section", None, None, "dp"),
            P("section", "dp", None),
            P(),
            P(None, "section"),
        ),
        out_specs=P(None, "win", "dp", None, "section"),
        check_vma=False,
    )
```
